512 devices in a mesh: depth: 64 (over z, y_lo, core), row: 8 (over y_hi, x).
Axes of the slice: x: 4, y: 4 (y_hi: 2, y_lo: 2; y = y_hi * 2 + y_lo), z: 16, core: 2. Of those that a mesh axis runs over, the one named last changes fastest.
Arguments:
- data: float32 [2, 192, 512, 512], P(None, 'depth', 'row'), may hold values from -0.25 to 0.25
- wavenumbers: float32 [512], replicated, may hold values from 0.3 to 3
- eps_rows: int32 [512], P('row'), may hold values from 1 to 2, as said below
- eps_cols: int32 [512], replicated, may hold values from 1 to 2, as said below
Outputs:
- prediction: float32 [2, 512, 512], P(None, 'row', 'depth')
The draws below stay inside these ranges and needn't reach their ends.
Inputs may be any that keep to these rules, and one draw needn't show every extreme that they name: `eps_rows`: each entry is a separation between 1 and 2; the value 2 occurs. `eps_cols`: each entry is a separation between 1 and 2; the value 2 occurs.
All inputs are finite; a program needn't handle non-finite values.
Results may differ from the reference program's by a relative error of at most 0.0003.
Values sent between devices are 32-bit elements; how exact they have to be, the bound alone decides.
No kernel may reach another device: no remote copies, remote signals or barrier semaphores. Data moves between devices by JAX's collectives and lax.ppermute only.
A program may use at most 64 MiB of HBM per device.

```python
import math
import jax
import jax.numpy as jnp
from jax import lax

W = 512
EPS_MOST = 2
DEPTH = 192


def draw_eps_rows(key, part):
    key = jax.random.fold_in(key, 11)
    values = jax.random.randint(key, (W,), 1, EPS_MOST + 1)
    place = jax.random.randint(jax.random.fold_in(key, 5), (), 0, W)
    return jnp.where(jnp.arange(W) == place, EPS_MOST, values).astype(jnp.int32)


def draw_eps_cols(key, part):
    key = jax.random.fold_in(key, 23)
    values = jax.random.randint(key, (W,), 1, EPS_MOST + 1)
    place = jax.random.randint(jax.random.fold_in(key, 9), (), 0, W)
    return jnp.where(jnp.arange(W) == place, EPS_MOST, values).astype(jnp.int32)


def shard_levels(own_key, shape, split, least, high):
    gain, own = 1.0, jax.random.fold_in(own_key, 6)
    for position, parts in split:
        heights = jnp.exp(jax.random.uniform(jax.random.fold_in(own, position), (parts,), jnp.float32, least / len(split), high / len(split)))
        gain = gain * jnp.repeat(heights, shape[position] // parts).reshape([-1 if axis == position else 1 for axis in range(len(shape))])
    return gain


def centred(stream_key, shape, spread, reach, pieces=(), held_as=jnp.bfloat16):
    drawn = spread * jax.random.normal(stream_key, shape, jnp.float32)
    if pieces:
        drawn = drawn * shard_levels(stream_key, shape, pieces, -0.22, 0.18)
    return jnp.clip(drawn, -reach, reach).astype(held_as)


def setup_inputs(seed: int = 0) -> dict:
    splits = jax.random.split(jax.random.key(seed), 5)
    data = centred(splits[0], (2, DEPTH, W, W), W ** -0.5, 0.25, ((1, 64), (2, 8)), jnp.float32)
    wavenumbers = jnp.clip(jnp.exp(jax.random.uniform(splits[1], (W,), jnp.float32, math.log(0.3), math.log(3.0))), 0.3, 3.0)
    eps_rows = draw_eps_rows(jax.random.fold_in(splits[4], 71), 0)
    eps_cols = draw_eps_cols(jax.random.fold_in(splits[4], 71), 0)
    return {"data": data, "wavenumbers": wavenumbers, "eps_rows": eps_rows, "eps_cols": eps_cols}


def complex_product(first_re, first_im, second_re, second_im):
    high = lax.Precision.HIGHEST
    real_part = jnp.dot(first_re, second_re, precision=high, preferred_element_type=jnp.float32) - jnp.dot(first_im, second_im, precision=high, preferred_element_type=jnp.float32)
    imag_part = jnp.dot(first_re, second_im, precision=high, preferred_element_type=jnp.float32) + jnp.dot(first_im, second_re, precision=high, preferred_element_type=jnp.float32)
    return real_part, imag_part


def reference(data, wavenumbers, eps_rows, eps_cols):
    levels = jnp.arange(DEPTH).astype(jnp.float32) + 0.5
    wave_sum = wavenumbers[:, None] + wavenumbers[None, :]
    phase = wave_sum[None, :, :] * levels[:, None, None]
    cosine = jnp.cos(phase)
    sine = jnp.sin(phase)
    real_data = data[0]
    imag_data = data[1]
    down_re = real_data * cosine - imag_data * sine
    down_im = real_data * sine + imag_data * cosine
    up_re = real_data * cosine + imag_data * sine
    up_im = imag_data * cosine - real_data * sine
    suffix_re = jnp.flip(jnp.cumsum(jnp.flip(down_re, 0), 0), 0)
    suffix_im = jnp.flip(jnp.cumsum(jnp.flip(down_im, 0), 0), 0)
    zero_slabs = jnp.zeros((EPS_MOST + 1, W, W), jnp.float32)
    padded_re = jnp.concatenate([suffix_re, zero_slabs], 0)
    padded_im = jnp.concatenate([suffix_im, zero_slabs], 0)

    def one_slab(total, inputs):
        slab, slab_up_re, slab_up_im = inputs
        window_re = lax.dynamic_slice_in_dim(padded_re, slab + 1, EPS_MOST + 1, 0)
        window_im = lax.dynamic_slice_in_dim(padded_im, slab + 1, EPS_MOST + 1, 0)
        left_re = jnp.zeros((W, W), jnp.float32)
        left_im = jnp.zeros((W, W), jnp.float32)
        right_re = jnp.zeros((W, W), jnp.float32)
        right_im = jnp.zeros((W, W), jnp.float32)
        for offset in range(1, EPS_MOST + 1):
            row_mask = (eps_rows == offset)[:, None]
            col_mask = (eps_cols == offset)[None, :]
            left_re = jnp.where(row_mask, window_re[offset], left_re)
            left_im = jnp.where(row_mask, window_im[offset], left_im)
            right_re = jnp.where(col_mask, window_re[offset], right_re)
            right_im = jnp.where(col_mask, window_im[offset], right_im)
        middle_re, middle_im = complex_product(left_re, left_im, slab_up_re, slab_up_im)
        term_re, term_im = complex_product(middle_re, middle_im, right_re, right_im)
        return (total[0] + term_re, total[1] + term_im), None

    start = (jnp.zeros((W, W), jnp.float32), jnp.zeros((W, W), jnp.float32))
    slabs = jnp.arange(DEPTH).astype(jnp.int32)
    final, unused = lax.scan(one_slab, start, (slabs, up_re, up_im))
    return jnp.stack([final[0], final[1]]) * (4.0 / DEPTH)
```

```python
import jax
import jax.numpy as jnp
from jax import lax
from jax.experimental import pallas as pl
from jax.experimental.pallas import tpu as pltpu
from jax.sharding import PartitionSpec as P

EPS_MOST = 2
CHUNK = 8
VMEM = pl.BlockSpec(memory_space=pltpu.VMEM)
SMEM = pl.BlockSpec(memory_space=pltpu.SMEM)
BIG = 40 * 1024 * 1024


def call(kernel, out_shape, *args, scratch=(), smem=(), flops=0):
    moved = sum(a.size * 4 for a in args) + 4 * out_shape.size
    return pl.pallas_call(
        kernel,
        out_shape=out_shape,
        in_specs=[SMEM if i in smem else VMEM for i in range(len(args))],
        out_specs=VMEM,
        scratch_shapes=list(scratch),
        compiler_params=pltpu.CompilerParams(vmem_limit_bytes=BIG),
        cost_estimate=pl.CostEstimate(flops=flops, bytes_accessed=moved, transcendentals=0),
    )(*args)


def suffix_kernel(parts, out):
    count = parts.shape[0]
    state = jnp.zeros(parts.shape[1:], jnp.float32)
    for place in range(count - 1, -1, -1):
        out[place] = state
        state = state + parts[place]


def factor_kernel(carry, down, up, rim, eps_r, eps_c, out):
    slabs = down.shape[1]
    near_row = eps_r[...] == 1
    near_col = eps_c[...] == 1
    for part in range(2):
        below = carry[part]
        for slab in range(slabs - 1, -1, -1):
            here = below + down[part, slab]
            out[slab, part] = jnp.where(near_row, here, below)
            out[slab, 2 + part] = rim[part, slab] if slab < EPS_MOST else up[part, slab - EPS_MOST]
            out[slab, 4 + part] = jnp.where(near_col, here, below)
            below = here
    for idle in range(slabs, out.shape[0]):
        out[idle] = jnp.zeros(out.shape[1:], jnp.float32)


def split(value):
    high = value.astype(jnp.bfloat16)
    return high, (value - high.astype(jnp.float32)).astype(jnp.bfloat16)


def real_dot(first, second):
    dot = lambda a, b: jnp.dot(a, b, preferred_element_type=jnp.float32)
    return dot(first[0], second[0]) + (dot(first[0], second[1]) + dot(first[1], second[0]))


def complex_dot(first, second):
    p = real_dot(first[0], second[0])
    q = real_dot(first[1], second[1])
    r = real_dot(first[2], second[2])
    return p - q, r - p - q


def triple(re, im):
    return split(re), split(im), split(re + im)


def product_kernel(core, own, other, out, mid, last):
    me = core[0]
    half = own.shape[-1]
    chips, rows = own.shape[0], own.shape[2] * CHUNK * 2

    def rows_of(ref, array, parity):
        return ref[:, array, :, parity].reshape(half, half)

    for column, ref in enumerate((own, other)):
        for block in range(2):
            parity = me if block == 0 else 1 - me
            both = triple(rows_of(ref, 2, parity), rows_of(ref, 3, parity))
            for kind in range(3):
                for level in range(2):
                    mid[kind, level, block * half : (block + 1) * half, column * half : (column + 1) * half] = both[kind][level]
    for block in range(2):
        parity = me if block == 0 else 1 - me
        both = triple(rows_of(own, 4, parity), rows_of(own, 5, parity))
        for kind in range(3):
            for level in range(2):
                last[kind, level, block * half : (block + 1) * half, :] = both[kind][level]
    second = [(mid[kind, 0], mid[kind, 1]) for kind in range(3)]
    third = [(last[kind, 0], last[kind, 1]) for kind in range(3)]
    step = 2
    for start in range(0, chips, step):
        pieces = slice(start, start + step)

        def left(array):
            near = own[pieces, array].reshape(step * rows, half)
            far = other[pieces, array].reshape(step * rows, half)
            return jnp.concatenate([near, far], axis=1)

        middle = complex_dot(triple(left(0), left(1)), second)
        result = complex_dot(triple(*middle), third)
        for part in range(2):
            out[pieces, part] = result[part].reshape(step, rows, half)


def turn_kernel(scale, parts, out):
    total = parts[0]
    for chip in range(1, 6):
        total = total + parts[chip]
    rows = jnp.concatenate([total[0], total[1]], axis=0) * scale
    out[...] = rows.T.reshape(out.shape)


def last_kernel(parts, out):
    total = jnp.sum(parts[...], axis=0)
    turned = total.T
    rows = out.shape[1]
    out[0] = turned[:rows]
    out[1] = turned[rows:]


def body(data, wavenumbers, eps_rows, eps_cols):
    slab_count, row_count, width = data.shape[1:]
    deep = lax.axis_size("depth")
    chips = lax.axis_size("row")
    pairs = deep // 2
    half = width // 2
    six = 2 * slab_count
    place = lax.axis_index("depth")
    core = place % 2
    pair = place // 2
    total_depth = slab_count * deep
    f32 = jnp.float32

    spot = jnp.arange(width)
    parity = jnp.where(spot < half, core, 1 - core)
    column = (spot % half) // CHUNK * (2 * CHUNK) + parity * CHUNK + spot % CHUNK
    chosen = (jnp.arange(width)[:, None] == column[None, :]).astype(f32)
    sorted_data = jnp.dot(data.reshape(-1, width), chosen, precision=lax.Precision.HIGHEST)
    kept = sorted_data[:, :half].reshape(2, slab_count, row_count, half)
    given = sorted_data[:, half:].reshape(2, slab_count, row_count, half)
    swap = [(i, i ^ 1) for i in range(deep)]
    taken = lax.ppermute(given, "depth", swap)
    first = jnp.where(core == 0, kept, taken)
    second = jnp.where(core == 0, taken, kept)
    slabs = jnp.concatenate([first, second], axis=1)

    row_waves = lax.dynamic_slice_in_dim(wavenumbers, lax.axis_index("row") * row_count, row_count)
    mine = lambda v: lax.dynamic_index_in_dim(v.reshape(pairs, 2, CHUNK), core, 1, False).reshape(half)
    col_waves = mine(wavenumbers)
    near_cols = mine(eps_cols)
    levels = (pair * six + jnp.arange(six)).astype(f32) + 0.5
    phase = (row_waves[:, None] + col_waves[None, :])[None] * levels[:, None, None]
    cosine, sine = jnp.cos(phase), jnp.sin(phase)
    down = jnp.stack([slabs[0] * cosine - slabs[1] * sine, slabs[0] * sine + slabs[1] * cosine])
    up = jnp.stack([slabs[0] * cosine + slabs[1] * sine, slabs[1] * cosine - slabs[0] * sine])
    rim = lax.ppermute(up[:, six - EPS_MOST :], "depth", [(i, i + 2) for i in range(deep - 2)])

    groups = [[2 * e + c for e in range(pairs)] for c in range(2)]
    spread = lambda v: lax.all_to_all(v, "depth", 0, 0, axis_index_groups=groups, tiled=True)
    totals = jnp.sum(down, axis=1)
    tiles = totals.reshape(2, row_count // 8, 8, half // 128, 128).transpose(0, 1, 3, 2, 4).reshape(pairs, 8, 128)
    seen = spread(tiles)
    sums = call(suffix_kernel, jax.ShapeDtypeStruct(seen.shape, f32), seen)
    back = spread(sums)
    carry = back.reshape(2, row_count // 8, half // 128, 8, 128).transpose(0, 1, 3, 2, 4).reshape(2, row_count, half)

    pieces = call(
        factor_kernel,
        jax.ShapeDtypeStruct((chips, 6, row_count, half), f32),
        carry, down, up, rim, eps_rows.reshape(row_count, 1), near_cols.reshape(1, half),
    )
    whole = lax.all_to_all(pieces, "row", 0, 0, tiled=True)
    other = lax.ppermute(whole[:, :4], "depth", swap)
    shape = lambda v: v.reshape(chips, v.shape[1], row_count // 16, 2, 8, half)
    partial = call(
        product_kernel,
        jax.ShapeDtypeStruct((chips, 2, row_count, half), f32),
        core.reshape(1).astype(jnp.int32), shape(whole), shape(other),
        smem=(0,),
        scratch=[pltpu.VMEM((3, 2, width, width), jnp.bfloat16), pltpu.VMEM((3, 2, width, half), jnp.bfloat16)],
        flops=18 * width * width * (width + half),
    )
    gathered = lax.all_to_all(partial, "row", 0, 0, tiled=True)
    turned = call(
        lambda parts, out: turn_kernel(4.0 / total_depth, parts, out),
        jax.ShapeDtypeStruct((pairs, CHUNK, 2 * row_count), f32),
        gathered,
    )
    ends = spread(turned)
    return call(last_kernel, jax.ShapeDtypeStruct((2, row_count, CHUNK), f32), ends)


def solution(mesh):
    in_specs = (P(None, "depth", "row", None), P(), P("row"), P())
    out_specs = P(None, "row", "depth")
    return jax.shard_map(body, mesh=mesh, in_specs=in_specs, out_specs=out_specs, check_vma=False)
```

```python
import jax
import jax.numpy as jnp
from jax import lax
from jax.experimental import pallas as pl
from jax.experimental.pallas import tpu as pltpu
from jax.sharding import PartitionSpec as P

EPS_MOST = 2
CHUNK = 8
SLABS = 6
NEAR = 8
VMEM = pl.BlockSpec(memory_space=pltpu.VMEM)
SMEM = pl.BlockSpec(memory_space=pltpu.SMEM)
MIB = 1024 * 1024
f32 = jnp.float32


def call(kernel, out_shape, *args, scratch=(), smem=(), flops=0, room=6):
    single = not isinstance(out_shape, list)
    shapes = [out_shape] if single else out_shape
    shapes = [s if hasattr(s, "dtype") else jax.ShapeDtypeStruct(s, f32) for s in shapes]
    moved = sum(a.size * 4 for a in args) + sum(4 * s.size for s in shapes)
    return pl.pallas_call(
        kernel,
        out_shape=shapes[0] if single else shapes,
        in_specs=[SMEM if i in smem else VMEM for i in range(len(args))],
        out_specs=VMEM if single else [VMEM] * len(shapes),
        scratch_shapes=list(scratch),
        compiler_params=pltpu.CompilerParams(vmem_limit_bytes=room * MIB),
        cost_estimate=pl.CostEstimate(flops=flops, bytes_accessed=moved, transcendentals=0),
    )(*args)


def phase_kernel(core, kept, taken, row_trig, col_trig, down, up, rim, total):
    first_core = core[0] == 0
    held = kept.shape[1]
    totals = [None, None]
    for slab in range(2 * held):
        local = slab % held
        pick = lambda part: (
            jnp.where(first_core, kept[part, local], taken[part, local])
            if slab < held
            else jnp.where(first_core, taken[part, local], kept[part, local])
        )
        re, im = pick(0), pick(1)
        row_cos, row_sin = row_trig[:, slab : slab + 1], row_trig[:, 8 + slab : 9 + slab]
        col_cos, col_sin = col_trig[slab : slab + 1, :], col_trig[8 + slab : 9 + slab, :]
        cosine = row_cos * col_cos - row_sin * col_sin
        sine = row_sin * col_cos + row_cos * col_sin
        a, b, c, d = re * cosine, im * sine, re * sine, im * cosine
        sums = (a - b, c + d)
        rises = (a + b, d - c)
        for part in range(2):
            down[part, slab] = sums[part]
            totals[part] = sums[part] if slab == 0 else totals[part] + sums[part]
            if slab < 2 * held - EPS_MOST:
                up[part, slab] = rises[part]
            else:
                rim[part, slab - 2 * held + EPS_MOST] = rises[part]
    for part in range(2):
        for block in range(8):
            for lane in range(2):
                tile = totals[part][8 * block : 8 * block + 8, 128 * lane : 128 * lane + 128]
                total[(8 * part + block) // 2, 2 * (block % 2) + lane] = tile


def early_kernel(down, up, rim, eps_r, eps_c, out):
    gap = (eps_c[...] == 1).astype(f32) - (eps_r[...] == 1).astype(f32)
    for slab in range(SLABS):
        for part in range(2):
            out[slab, part] = rim[part, slab] if slab < EPS_MOST else up[part, slab - EPS_MOST]
            out[slab, 2 + part] = down[part, slab] * gap
    for idle in range(SLABS, out.shape[0]):
        out[idle] = jnp.zeros(out.shape[1:], f32)


def group_kernel(parts, out, total):
    state = parts[parts.shape[0] - 1]
    out[parts.shape[0] - 1] = jnp.zeros(parts.shape[1:], f32)
    for place in range(parts.shape[0] - 2, -1, -1):
        out[place] = state
        state = state + parts[place]
    total[...] = state


def deep_kernel(sums, *refs):
    deeper, out = refs[:-1], refs[-1]
    extra = deeper[0][...]
    for other in deeper[1:]:
        extra = extra + other[...]
    for place in range(sums.shape[0]):
        out[place] = sums[place] + extra


def late_kernel(carry, down, eps_r, out):
    near_row = eps_r[...] == 1
    for part in range(2):
        for block in range(8):
            rows = slice(8 * block, 8 * block + 8)
            for lane in range(2):
                cols = slice(128 * lane, 128 * lane + 128)
                below = carry[(8 * part + block) // 2, 2 * (block % 2) + lane]
                for slab in range(SLABS - 1, -1, -1):
                    here = below + down[part, slab, rows, cols]
                    out[slab, part, rows, cols] = jnp.where(near_row[rows], here, below)
                    below = here
    for idle in range(SLABS, out.shape[0]):
        out[idle] = jnp.zeros(out.shape[1:], f32)


def split(value):
    high = value.astype(jnp.bfloat16)
    return high, (value - high.astype(f32)).astype(jnp.bfloat16)


def real_dot(first, second):
    dot = lambda a, b: jnp.dot(a, b, preferred_element_type=f32)
    return dot(first[0], second[0]) + (dot(first[0], second[1]) + dot(first[1], second[0]))


def complex_dot(first, second):
    p = real_dot(first[0], second[0])
    q = real_dot(first[1], second[1])
    r = real_dot(first[2], second[2])
    return p - q, r - p - q


def triple(re, im):
    return split(re), split(im), split(re + im)


def ready_kernel(core, own, far, mid):
    half = own.shape[-1]
    for block in range(2):
        parity = core[0] if block == 0 else 1 - core[0]
        stretch = slice(block * half, block * half + half)
        for column, ref in enumerate((own, far)):
            both = triple(*(ref[:, part, :, parity].reshape(half, half) for part in range(2)))
            for kind in range(3):
                for level in range(2):
                    mid[kind, level, stretch, column * half : (column + 1) * half] = both[kind][level]


def product_kernel(core, own, far, early, mid, out, last):
    half = out.shape[-1]
    chips, rows = out.shape[0], out.shape[2]
    for block in range(2):
        parity = core[0] if block == 0 else 1 - core[0]
        stretch = slice(block * half, block * half + half)
        both = triple(*((own[:, part, :, parity] + early[:, 2 + part, :, parity]).reshape(half, half) for part in range(2)))
        for kind in range(3):
            for level in range(2):
                last[kind, level, stretch, :] = both[kind][level]
    second = [(mid[kind, 0], mid[kind, 1]) for kind in range(3)]
    third = [(last[kind, 0], last[kind, 1]) for kind in range(3)]
    step = 2
    for start in range(0, chips, step):
        pieces = slice(start, start + step)
        left = [jnp.concatenate([ref[pieces, part].reshape(step * rows, half) for ref in (own, far)], axis=1) for part in range(2)]
        middle = complex_dot(triple(*left), second)
        result = complex_dot(triple(*middle), third)
        for part in range(2):
            out[pieces, part] = result[part].reshape(step, rows, half)


def turn_kernel(scale, parts, out):
    total = parts[0]
    for chip in range(1, SLABS):
        total = total + parts[chip]
    turned = (jnp.concatenate([total[0], total[1]], axis=0) * scale).T
    out[...] = turned.reshape(out.shape)


def last_kernel(parts, out):
    total = parts[0]
    for place in range(1, parts.shape[0]):
        total = total + parts[place]
    turned = total.T
    rows = out.shape[1]
    out[0] = turned[:rows]
    out[1] = turned[rows:]


def body(data, wavenumbers, eps_rows, eps_cols):
    slab_count, row_count, width = data.shape[1:]
    deep = lax.axis_size("depth")
    chips = lax.axis_size("row")
    pairs = deep // 2
    half = width // 2
    place = lax.axis_index("depth")
    core = place % 2
    pair = place // 2
    total_depth = slab_count * deep
    me = core.reshape(1).astype(jnp.int32)

    spot = jnp.arange(width)
    parity = jnp.where(spot < half, core, 1 - core)
    column = (spot % half) // CHUNK * (2 * CHUNK) + parity * CHUNK + spot % CHUNK
    chosen = (jnp.arange(width)[:, None] == column[None, :]).astype(f32)
    sorted_data = jnp.dot(data.reshape(-1, width), chosen, precision=lax.Precision.HIGHEST)
    kept = sorted_data[:, :half].reshape(2, slab_count, row_count, half)
    given = sorted_data[:, half:].reshape(2, slab_count, row_count, half)
    swap = [(i, i ^ 1) for i in range(deep)]
    taken = lax.ppermute(given, "depth", swap)

    row_waves = lax.dynamic_slice_in_dim(wavenumbers, lax.axis_index("row") * row_count, row_count)
    mine = lambda v: lax.dynamic_index_in_dim(v.reshape(pairs, 2, CHUNK), core, 1, False).reshape(half)
    col_waves = mine(wavenumbers)
    near_cols = mine(eps_cols).reshape(1, half)
    levels = (pair * SLABS + jnp.arange(8)).astype(f32) + 0.5
    row_phase = row_waves[:, None] * levels[None, :]
    col_phase = levels[:, None] * col_waves[None, :]
    row_trig = jnp.concatenate([jnp.cos(row_phase), jnp.sin(row_phase)], axis=1)
    col_trig = jnp.concatenate([jnp.cos(col_phase), jnp.sin(col_phase)], axis=0)
    down, up, rim, total = call(
        phase_kernel,
        [
            (2, SLABS, row_count, half),
            (2, SLABS - EPS_MOST, row_count, half),
            (2, EPS_MOST, row_count, half),
            (NEAR, 32 // NEAR, 8, 128),
        ],
        me, kept, taken, row_trig, col_trig,
        smem=(0,),
        room=10,
    )

    near = [[2 * (g * NEAR + i) + c for i in range(NEAR)] for g in range(pairs // NEAR) for c in range(2)]
    spread = lambda v, groups: lax.all_to_all(v, "depth", 0, 0, axis_index_groups=groups, tiled=True)
    seen = spread(total, near)
    sums, group = call(group_kernel, [seen.shape, seen.shape[1:]], seen)
    deeper = [
        lax.ppermute(group, "depth", [(i, i - shift) for i in range(shift, deep)])
        for shift in range(2 * NEAR, deep, 2 * NEAR)
    ]

    rim = lax.ppermute(rim, "depth", [(i, i + 2) for i in range(deep - 2)])
    row_marks = eps_rows.reshape(row_count, 1)
    early = call(early_kernel, (chips, 4, row_count, half), down, up, rim, row_marks, near_cols)
    early = lax.all_to_all(early, "row", 0, 0, tiled=True)
    early, *deeper = lax.optimization_barrier((early, *deeper))
    carry = spread(call(deep_kernel, sums.shape, sums, *deeper), near)
    early_far = lax.ppermute(early, "depth", swap)
    shape = lambda v: v.reshape(chips, v.shape[1], row_count // 16, 2, 8, half)
    mid = call(
        ready_kernel,
        jax.ShapeDtypeStruct((3, 2, width, width), jnp.bfloat16),
        me, shape(early), shape(early_far),
        smem=(0,),
        room=12,
    )

    whole = (chips, 2, row_count, half)
    late = call(late_kernel, whole, carry, down, row_marks)
    left = lax.all_to_all(late, "row", 0, 0, tiled=True)
    left_far = lax.ppermute(left, "depth", swap)
    partial = call(
        product_kernel,
        whole,
        me, shape(left), shape(left_far), shape(early), mid,
        smem=(0,),
        scratch=[pltpu.VMEM((3, 2, width, half), jnp.bfloat16)],
        flops=18 * width * width * (width + half),
        room=20,
    )
    gathered = lax.all_to_all(partial, "row", 0, 0, tiled=True)
    turned = call(
        lambda parts, out: turn_kernel(4.0 / total_depth, parts, out),
        (pairs, CHUNK, 2 * row_count),
        gathered,
    )
    ends = spread(turned, [[2 * e + c for e in range(pairs)] for c in range(2)])
    return call(last_kernel, (2, row_count, CHUNK), ends)


def solution(mesh):
    in_specs = (P(None, "depth", "row", None), P(), P("row"), P())
    out_specs = P(None, "row", "depth")
    return jax.shard_map(body, mesh=mesh, in_specs=in_specs, out_specs=out_specs, check_vma=False)
```

```python
import jax
import jax.numpy as jnp
from jax import lax
from jax.experimental import pallas as pl
from jax.experimental.pallas import tpu as pltpu
from jax.sharding import PartitionSpec as P

EPS_MOST = 2
CHUNK = 8
SLABS = 6
NEAR = 8
VMEM = pl.BlockSpec(memory_space=pltpu.VMEM)
SMEM = pl.BlockSpec(memory_space=pltpu.SMEM)
HBM = pl.BlockSpec(memory_space=pltpu.HBM)
MIB = 1024 * 1024
f32 = jnp.float32


def call(kernel, out_shape, *args, scratch=(), smem=(), hbm=(), flops=0, room=6):
    single = not isinstance(out_shape, list)
    shapes = [out_shape] if single else out_shape
    shapes = [s if hasattr(s, "dtype") else jax.ShapeDtypeStruct(s, f32) for s in shapes]
    moved = sum(a.size * 4 for a in args) + sum(4 * s.size for s in shapes)
    return pl.pallas_call(
        kernel,
        out_shape=shapes[0] if single else shapes,
        in_specs=[SMEM if i in smem else HBM if i in hbm else VMEM for i in range(len(args))],
        out_specs=VMEM if single else [VMEM] * len(shapes),
        scratch_shapes=list(scratch),
        compiler_params=pltpu.CompilerParams(vmem_limit_bytes=room * MIB),
        cost_estimate=pl.CostEstimate(flops=flops, bytes_accessed=moved, transcendentals=0),
    )(*args)


def turned(row_trig, col_trig, level):
    row_cos, row_sin = row_trig[:, level : level + 1], row_trig[:, 8 + level : 9 + level]
    col_cos, col_sin = col_trig[level : level + 1, :], col_trig[8 + level : 9 + level, :]
    return row_cos * col_cos - row_sin * col_sin, row_sin * col_cos + row_cos * col_sin


def phase_kernel(core, kept, taken, row_trig, col_trig, down, up, rim, total):
    first_core = core[0] == 0
    held = kept.shape[1]
    totals = [None, None]
    for slab in range(2 * held):
        local = slab % held
        pick = lambda part: (
            jnp.where(first_core, kept[part, local], taken[part, local])
            if slab < held
            else jnp.where(first_core, taken[part, local], kept[part, local])
        )
        re, im = pick(0), pick(1)
        cosine, sine = turned(row_trig, col_trig, slab)
        a, b, c, d = re * cosine, im * sine, re * sine, im * cosine
        sums = (a - b, c + d)
        rises = (a + b, d - c)
        for part in range(2):
            down[part, slab] = sums[part]
            totals[part] = sums[part] if slab == 0 else totals[part] + sums[part]
            if slab < 2 * held - EPS_MOST:
                up[part, slab] = rises[part]
            else:
                rim[part, slab - 2 * held + EPS_MOST] = rises[part]
    for part in range(2):
        for block in range(8):
            for lane in range(2):
                tile = totals[part][8 * block : 8 * block + 8, 128 * lane : 128 * lane + 128]
                total[(8 * part + block) // 2, 2 * (block % 2) + lane] = tile


def group_kernel(parts, out, total):
    state = parts[parts.shape[0] - 1]
    out[parts.shape[0] - 1] = jnp.zeros(parts.shape[1:], f32)
    for place in range(parts.shape[0] - 2, -1, -1):
        out[place] = state
        state = state + parts[place]
    total[...] = state


def deep_kernel(sums, *refs):
    deeper, out = refs[:-1], refs[-1]
    extra = deeper[0][...]
    for other in deeper[1:]:
        extra = extra + other[...]
    for place in range(sums.shape[0]):
        out[place] = sums[place] + extra


def late_kernel(carry, down, up, rim, eps_r, eps_c, out):
    near_row = eps_r[...] == 1
    for part in range(2):
        for slab in range(SLABS):
            out[slab, 2 + part] = rim[part, slab] if slab < EPS_MOST else up[part, slab - EPS_MOST]
        for block in range(8):
            rows = slice(8 * block, 8 * block + 8)
            for lane in range(2):
                cols = slice(128 * lane, 128 * lane + 128)
                near_col = eps_c[:, cols] == 1
                below = carry[(8 * part + block) // 2, 2 * (block % 2) + lane]
                for slab in range(SLABS - 1, -1, -1):
                    here = below + down[part, slab, rows, cols]
                    out[slab, part, rows, cols] = jnp.where(near_row[rows], here, below)
                    out[slab, 4 + part, rows, cols] = jnp.where(near_col, here, below)
                    below = here
    for idle in range(SLABS, out.shape[0]):
        out[idle] = jnp.zeros(out.shape[1:], f32)


def split(value):
    high = value.astype(jnp.bfloat16)
    return high, (value - high.astype(f32)).astype(jnp.bfloat16)


def real_dot(first, second):
    dot = lambda a, b: jnp.dot(a, b, preferred_element_type=f32)
    return dot(first[0], second[0]) + (dot(first[0], second[1]) + dot(first[1], second[0]))


def complex_dot(first, second):
    p = real_dot(first[0], second[0])
    q = real_dot(first[1], second[1])
    r = real_dot(first[2], second[2])
    return p - q, r - p - q


def triple(re, im):
    return split(re), split(im), split(re + im)


def right_kernel(core, whole, right):
    half = right.shape[-1]
    for block, parity in enumerate((core[0], 1 - core[0])):
        stretch = slice(block * half, block * half + half)
        both = triple(*(whole[:, 4 + part, :, parity].reshape(half, half) for part in range(2)))
        for kind in range(3):
            for level in range(2):
                right[kind, level, stretch, :] = both[kind][level]


def first_kernel(core, own, far, right, out):
    half = out.shape[-1]
    second = [(right[kind, 0], right[kind, 1]) for kind in range(3)]
    step = half // 2
    for block, parity in enumerate((core[0], 1 - core[0])):
        for start in range(0, 2):
            pieces = slice(4 * start, 4 * start + 4)
            rises = [
                jnp.concatenate([ref[pieces, 2 + part, :, parity].reshape(step, half) for ref in (own, far)], axis=1)
                for part in range(2)
            ]
            both = triple(*complex_dot(triple(*rises), second))
            rows = slice(block * half + start * step, block * half + start * step + step)
            for kind in range(3):
                for level in range(2):
                    out[kind, level, rows] = both[kind][level]


def second_kernel(own, far, middle, out):
    half = out.shape[-1]
    chips, rows = out.shape[0], out.shape[2]
    second = [(middle[kind, 0], middle[kind, 1]) for kind in range(3)]
    step = 2
    for start in range(0, chips, step):
        pieces = slice(start, start + step)
        left = [jnp.concatenate([ref[pieces, part].reshape(step * rows, half) for ref in (own, far)], axis=1) for part in range(2)]
        result = complex_dot(triple(*left), second)
        for part in range(2):
            out[pieces, part] = result[part].reshape(step, rows, half)


def turn_kernel(scale, parts, out):
    total = parts[0]
    for chip in range(1, SLABS):
        total = total + parts[chip]
    turned = (jnp.concatenate([total[0], total[1]], axis=0) * scale).T
    out[...] = turned.reshape(out.shape)


def last_kernel(parts, out):
    total = parts[0]
    for place in range(1, parts.shape[0]):
        total = total + parts[place]
    turned = total.T
    rows = out.shape[1]
    out[0] = turned[:rows]
    out[1] = turned[rows:]


def body(data, wavenumbers, eps_rows, eps_cols):
    slab_count, row_count, width = data.shape[1:]
    deep = lax.axis_size("depth")
    chips = lax.axis_size("row")
    pairs = deep // 2
    half = width // 2
    place = lax.axis_index("depth")
    core = place % 2
    pair = place // 2
    total_depth = slab_count * deep
    me = core.reshape(1).astype(jnp.int32)

    spot = jnp.arange(width)
    parity = jnp.where(spot < half, core, 1 - core)
    column = (spot % half) // CHUNK * (2 * CHUNK) + parity * CHUNK + spot % CHUNK
    chosen = (jnp.arange(width)[:, None] == column[None, :]).astype(f32)
    sorted_data = jnp.dot(data.reshape(-1, width), chosen, precision=lax.Precision.HIGHEST)
    kept = sorted_data[:, :half].reshape(2, slab_count, row_count, half)
    given = sorted_data[:, half:].reshape(2, slab_count, row_count, half)
    swap = [(i, i ^ 1) for i in range(deep)]
    taken = lax.ppermute(given, "depth", swap)

    row_waves = lax.dynamic_slice_in_dim(wavenumbers, lax.axis_index("row") * row_count, row_count)
    mine = lambda v: lax.dynamic_index_in_dim(v.reshape(pairs, 2, CHUNK), core, 1, False).reshape(half)
    col_waves = mine(wavenumbers)
    near_cols = mine(eps_cols).reshape(1, half)
    levels = (pair * SLABS + jnp.arange(8)).astype(f32) + 0.5
    row_phase = row_waves[:, None] * levels[None, :]
    col_phase = levels[:, None] * col_waves[None, :]
    row_trig = jnp.concatenate([jnp.cos(row_phase), jnp.sin(row_phase)], axis=1)
    col_trig = jnp.concatenate([jnp.cos(col_phase), jnp.sin(col_phase)], axis=0)
    down, up, rim, total = call(
        phase_kernel,
        [
            (2, SLABS, row_count, half),
            (2, SLABS - EPS_MOST, row_count, half),
            (2, EPS_MOST, row_count, half),
            (NEAR, 32 // NEAR, 8, 128),
        ],
        me, kept, taken, row_trig, col_trig,
        smem=(0,),
        room=10,
    )

    near = [[2 * (g * NEAR + i) + c for i in range(NEAR)] for g in range(pairs // NEAR) for c in range(2)]
    spread = lambda v, groups: lax.all_to_all(v, "depth", 0, 0, axis_index_groups=groups, tiled=True)
    seen = spread(total, near)
    sums, group = call(group_kernel, [seen.shape, seen.shape[1:]], seen)
    deeper = [
        lax.ppermute(group, "depth", [(i, i - shift) for i in range(shift, deep)])
        for shift in range(2 * NEAR, deep, 2 * NEAR)
    ]
    rim = lax.ppermute(rim, "depth", [(i, i + 2) for i in range(deep - 2)])
    rim, *deeper = lax.optimization_barrier((rim, *deeper))
    carry = spread(call(deep_kernel, sums.shape, sums, *deeper), near)

    late = call(
        late_kernel,
        (chips, 6, row_count, half),
        carry, down, up, rim, eps_rows.reshape(row_count, 1), near_cols,
    )
    whole = lax.all_to_all(late, "row", 0, 0, tiled=True)
    other = lax.ppermute(whole[:, :4], "depth", swap)
    shape = lambda v: v.reshape(chips, v.shape[1], row_count // 16, 2, 8, half)
    parts = lambda n: jax.ShapeDtypeStruct((3, 2, width, n), jnp.bfloat16)
    right = call(right_kernel, parts(half), me, shape(whole), smem=(0,), room=8)
    middle = call(
        first_kernel,
        parts(half),
        me, shape(whole), shape(other), right,
        smem=(0,),
        flops=18 * width * width * half,
        room=12,
    )
    partial = call(
        second_kernel,
        (chips, 2, row_count, half),
        whole, other, middle,
        flops=18 * width * width * half,
        room=12,
    )
    gathered = lax.all_to_all(partial, "row", 0, 0, tiled=True)
    turned = call(
        lambda parts, out: turn_kernel(4.0 / total_depth, parts, out),
        (pairs, CHUNK, 2 * row_count),
        gathered,
    )
    ends = spread(turned, [[2 * e + c for e in range(pairs)] for c in range(2)])
    return call(last_kernel, (2, row_count, CHUNK), ends)


def solution(mesh):
    in_specs = (P(None, "depth", "row", None), P(), P("row"), P())
    out_specs = P(None, "row", "depth")
    return jax.shard_map(body, mesh=mesh, in_specs=in_specs, out_specs=out_specs, check_vma=False)
```

```python
import jax
import jax.numpy as jnp
from jax import lax
from jax.experimental import pallas as pl
from jax.experimental.pallas import tpu as pltpu
from jax.sharding import PartitionSpec as P

EPS_MOST = 2
CHUNK = 8
SLABS = 6
NEAR = 8
VMEM = pl.BlockSpec(memory_space=pltpu.VMEM)
SMEM = pl.BlockSpec(memory_space=pltpu.SMEM)
HBM = pl.BlockSpec(memory_space=pltpu.HBM)
MIB = 1024 * 1024
f32 = jnp.float32


def call(kernel, out_shape, *args, scratch=(), smem=(), hbm=(), flops=0, room=6):
    single = not isinstance(out_shape, list)
    shapes = [out_shape] if single else out_shape
    shapes = [s if hasattr(s, "dtype") else jax.ShapeDtypeStruct(s, f32) for s in shapes]
    moved = sum(a.size * 4 for a in args) + sum(4 * s.size for s in shapes)
    return pl.pallas_call(
        kernel,
        out_shape=shapes[0] if single else shapes,
        in_specs=[SMEM if i in smem else HBM if i in hbm else VMEM for i in range(len(args))],
        out_specs=VMEM if single else [VMEM] * len(shapes),
        scratch_shapes=list(scratch),
        compiler_params=pltpu.CompilerParams(vmem_limit_bytes=room * MIB),
        cost_estimate=pl.CostEstimate(flops=flops, bytes_accessed=moved, transcendentals=0),
    )(*args)


def turned(row_trig, col_trig, level):
    row_cos, row_sin = row_trig[:, level : level + 1], row_trig[:, 8 + level : 9 + level]
    col_cos, col_sin = col_trig[level : level + 1, :], col_trig[8 + level : 9 + level, :]
    return row_cos * col_cos - row_sin * col_sin, row_sin * col_cos + row_cos * col_sin


def phase_kernel(core, kept, taken, row_trig, col_trig, down, up, rim, total):
    first_core = core[0] == 0
    held = kept.shape[1]
    totals = [None, None]
    for slab in range(2 * held):
        local = slab % held
        pick = lambda part: (
            jnp.where(first_core, kept[part, local], taken[part, local])
            if slab < held
            else jnp.where(first_core, taken[part, local], kept[part, local])
        )
        re, im = pick(0), pick(1)
        cosine, sine = turned(row_trig, col_trig, slab)
        a, b, c, d = re * cosine, im * sine, re * sine, im * cosine
        sums = (a - b, c + d)
        rises = (a + b, d - c)
        for part in range(2):
            down[part, slab] = sums[part]
            totals[part] = sums[part] if slab == 0 else totals[part] + sums[part]
            if slab < 2 * held - EPS_MOST:
                up[part, slab] = rises[part]
            else:
                rim[part, slab - 2 * held + EPS_MOST] = rises[part]
    for part in range(2):
        for block in range(8):
            for lane in range(2):
                tile = totals[part][8 * block : 8 * block + 8, 128 * lane : 128 * lane + 128]
                total[(8 * part + block) // 2, 2 * (block % 2) + lane] = tile


def group_kernel(parts, out, total):
    state = parts[parts.shape[0] - 1]
    out[parts.shape[0] - 1] = jnp.zeros(parts.shape[1:], f32)
    for place in range(parts.shape[0] - 2, -1, -1):
        out[place] = state
        state = state + parts[place]
    total[...] = state


def deep_kernel(sums, *refs):
    deeper, out = refs[:-1], refs[-1]
    extra = deeper[0][...]
    for other in deeper[1:]:
        extra = extra + other[...]
    for place in range(sums.shape[0]):
        out[place] = sums[place] + extra


def late_kernel(carry, down, up, rim, eps_r, eps_c, out):
    near_row = eps_r[...] == 1
    for part in range(2):
        for slab in range(SLABS):
            out[slab, 2 + part] = rim[part, slab] if slab < EPS_MOST else up[part, slab - EPS_MOST]
        for block in range(8):
            rows = slice(8 * block, 8 * block + 8)
            for lane in range(2):
                cols = slice(128 * lane, 128 * lane + 128)
                near_col = eps_c[:, cols] == 1
                below = carry[(8 * part + block) // 2, 2 * (block % 2) + lane]
                for slab in range(SLABS - 1, -1, -1):
                    here = below + down[part, slab, rows, cols]
                    out[slab, part, rows, cols] = jnp.where(near_row[rows], here, below)
                    out[slab, 4 + part, rows, cols] = jnp.where(near_col, here, below)
                    below = here
    for idle in range(SLABS, out.shape[0]):
        out[idle] = jnp.zeros(out.shape[1:], f32)


def split(value):
    high = value.astype(jnp.bfloat16)
    return high, (value - high.astype(f32)).astype(jnp.bfloat16)


def real_dot(first, second):
    dot = lambda a, b: jnp.dot(a, b, preferred_element_type=f32)
    return dot(first[0], second[0]) + (dot(first[0], second[1]) + dot(first[1], second[0]))


def complex_dot(first, second):
    p = real_dot(first[0], second[0])
    q = real_dot(first[1], second[1])
    r = real_dot(first[2], second[2])
    return p - q, r - p - q


def triple(re, im):
    return split(re), split(im), split(re + im)


def right_kernel(core, whole, right):
    half = right.shape[-1]
    step = half // 2
    for block, parity in enumerate((core[0], 1 - core[0])):
        for line in range(2):
            rows = slice(block * half + line * step, block * half + line * step + step)
            both = triple(*(whole[:, 4 + part, :, line, parity].reshape(step, half) for part in range(2)))
            for kind in range(3):
                for level in range(2):
                    right[kind, level, rows, :] = both[kind][level]


def first_kernel(core, own, far, right, out):
    half = out.shape[-1]
    second = [(right[kind, 0], right[kind, 1]) for kind in range(3)]
    step = half // 2
    for block, parity in enumerate((core[0], 1 - core[0])):
        for line in range(2):
            rises = [
                jnp.concatenate([ref[:, 2 + part, :, line, parity].reshape(step, half) for ref in (own, far)], axis=1)
                for part in range(2)
            ]
            both = triple(*complex_dot(triple(*rises), second))
            rows = slice(block * half + line * step, block * half + line * step + step)
            for kind in range(3):
                for level in range(2):
                    out[kind, level, rows] = both[kind][level]


def second_kernel(own, far, middle, out):
    quarter = out.shape[-1]
    half = 2 * quarter
    chips, rows = own.shape[0], own.shape[2]
    second = [(middle[kind, 0], middle[kind, 1]) for kind in range(3)]
    step = 2
    for start in range(0, chips, step):
        pieces = slice(start, start + step)
        left = [jnp.concatenate([ref[pieces, part].reshape(step * rows, half) for ref in (own, far)], axis=1) for part in range(2)]
        result = complex_dot(triple(*left), second)
        for part in range(2):
            value = result[part].reshape(step, rows, half)
            for line in range(2):
                out[line, pieces, part] = value[:, :, line * quarter : line * quarter + quarter]


def turn_kernel(scale, chips, parts, out):
    total = None
    for place in range(parts.shape[0]):
        if place % chips < SLABS:
            total = parts[place] if total is None else total + parts[place]
    turned = (jnp.concatenate([total[0], total[1]], axis=0) * scale).T
    out[...] = turned.reshape(out.shape)


def last_kernel(parts, out):
    total = parts[0]
    for place in range(1, parts.shape[0]):
        total = total + parts[place]
    turned = total.T
    rows = out.shape[1]
    out[0] = turned[:rows]
    out[1] = turned[rows:]


def body(data, wavenumbers, eps_rows, eps_cols):
    slab_count, row_count, width = data.shape[1:]
    deep = lax.axis_size("depth")
    chips = lax.axis_size("row")
    pairs = deep // 2
    half = width // 2
    place = lax.axis_index("depth")
    core = place % 2
    pair = place // 2
    total_depth = slab_count * deep
    me = core.reshape(1).astype(jnp.int32)

    planes = pairs // 2
    spot = jnp.arange(width)
    parity = jnp.where(spot < half, core, 1 - core)
    line, plane = spot % half // (half // 2), spot % (half // 2) // CHUNK
    column = ((plane * 2 + line) * 2 + parity) * CHUNK + spot % CHUNK
    chosen = (jnp.arange(width)[:, None] == column[None, :]).astype(f32)
    sorted_data = jnp.dot(data.reshape(-1, width), chosen, precision=lax.Precision.HIGHEST)
    kept = sorted_data[:, :half].reshape(2, slab_count, row_count, half)
    given = sorted_data[:, half:].reshape(2, slab_count, row_count, half)
    swap = [(i, i ^ 1) for i in range(deep)]
    taken = lax.ppermute(given, "depth", swap)

    row_waves = lax.dynamic_slice_in_dim(wavenumbers, lax.axis_index("row") * row_count, row_count)
    mine = lambda v: jnp.sum(chosen[:, :half] * v[:, None], axis=0)
    col_waves = mine(wavenumbers)
    near_cols = mine(eps_cols.astype(f32)).astype(jnp.int32).reshape(1, half)
    levels = (pair * SLABS + jnp.arange(8)).astype(f32) + 0.5
    row_phase = row_waves[:, None] * levels[None, :]
    col_phase = levels[:, None] * col_waves[None, :]
    row_trig = jnp.concatenate([jnp.cos(row_phase), jnp.sin(row_phase)], axis=1)
    col_trig = jnp.concatenate([jnp.cos(col_phase), jnp.sin(col_phase)], axis=0)
    down, up, rim, total = call(
        phase_kernel,
        [
            (2, SLABS, row_count, half),
            (2, SLABS - EPS_MOST, row_count, half),
            (2, EPS_MOST, row_count, half),
            (NEAR, 32 // NEAR, 8, 128),
        ],
        me, kept, taken, row_trig, col_trig,
        smem=(0,),
        room=10,
    )

    near = [[2 * (g * NEAR + i) + c for i in range(NEAR)] for g in range(pairs // NEAR) for c in range(2)]
    spread = lambda v, groups: lax.all_to_all(v, "depth", 0, 0, axis_index_groups=groups, tiled=True)
    seen = spread(total, near)
    sums, group = call(group_kernel, [seen.shape, seen.shape[1:]], seen)
    deeper = [
        lax.ppermute(group, "depth", [(i, i - shift) for i in range(shift, deep)])
        for shift in range(2 * NEAR, deep, 2 * NEAR)
    ]
    rim = lax.ppermute(rim, "depth", [(i, i + 2) for i in range(deep - 2)])
    rim, *deeper = lax.optimization_barrier((rim, *deeper))
    carry = spread(call(deep_kernel, sums.shape, sums, *deeper), near)

    late = call(
        late_kernel,
        (chips, 6, row_count, half),
        carry, down, up, rim, eps_rows.reshape(row_count, 1), near_cols,
    )
    whole = lax.all_to_all(late, "row", 0, 0, tiled=True)
    other = lax.ppermute(whole[:, :4], "depth", swap)
    shape = lambda v: v.reshape(chips, v.shape[1], row_count // 32, 2, 2, CHUNK, half)
    parts = lambda n: jax.ShapeDtypeStruct((3, 2, width, n), jnp.bfloat16)
    right = call(right_kernel, parts(half), me, shape(whole), smem=(0,), room=8)
    middle = call(
        first_kernel,
        parts(half),
        me, shape(whole), shape(other), right,
        smem=(0,),
        flops=18 * width * width * half,
        room=12,
    )
    partial = call(
        second_kernel,
        (2, chips, 2, row_count, half // 2),
        whole, other, middle,
        flops=18 * width * width * half,
        room=12,
    )
    in_plane = [
        [(4 * z + 2 * line + c) * chips + chip for line in range(2) for chip in range(chips)] for z in range(planes) for c in range(2)
    ]
    partial = partial.reshape(2 * chips, 2, row_count, half // 2)
    gathered = lax.all_to_all(partial, ("depth", "row"), 0, 0, axis_index_groups=in_plane, tiled=True)
    turned = call(
        lambda parts, out: turn_kernel(4.0 / total_depth, chips, parts, out),
        (planes, CHUNK, 2 * row_count),
        gathered,
    )
    ends = spread(turned, [[4 * z + k for z in range(planes)] for k in range(4)])
    return call(last_kernel, (2, row_count, CHUNK), ends)


def solution(mesh):
    in_specs = (P(None, "depth", "row", None), P(), P("row"), P())
    out_specs = P(None, "row", "depth")
    return jax.shard_map(body, mesh=mesh, in_specs=in_specs, out_specs=out_specs, check_vma=False)
```

```python
import jax
import jax.numpy as jnp
from jax import lax
from jax.experimental import pallas as pl
from jax.experimental.pallas import tpu as pltpu
from jax.sharding import PartitionSpec as P

EPS_MOST = 2
CHUNK = 8
SLABS = 6
NEAR = 8
VMEM = pl.BlockSpec(memory_space=pltpu.VMEM)
SMEM = pl.BlockSpec(memory_space=pltpu.SMEM)
HBM = pl.BlockSpec(memory_space=pltpu.HBM)
MIB = 1024 * 1024
f32 = jnp.float32


def call(kernel, out_shape, *args, scratch=(), smem=(), hbm=(), flops=0, room=6):
    single = not isinstance(out_shape, list)
    shapes = [out_shape] if single else out_shape
    shapes = [s if hasattr(s, "dtype") else jax.ShapeDtypeStruct(s, f32) for s in shapes]
    moved = sum(a.size * 4 for a in args) + sum(4 * s.size for s in shapes)
    return pl.pallas_call(
        kernel,
        out_shape=shapes[0] if single else shapes,
        in_specs=[SMEM if i in smem else HBM if i in hbm else VMEM for i in range(len(args))],
        out_specs=VMEM if single else [VMEM] * len(shapes),
        scratch_shapes=list(scratch),
        compiler_params=pltpu.CompilerParams(vmem_limit_bytes=room * MIB),
        cost_estimate=pl.CostEstimate(flops=flops, bytes_accessed=moved, transcendentals=0),
    )(*args)


def turned(row_trig, col_trig, level):
    row_cos, row_sin = row_trig[:, level : level + 1], row_trig[:, 8 + level : 9 + level]
    col_cos, col_sin = col_trig[level : level + 1, :], col_trig[8 + level : 9 + level, :]
    return row_cos * col_cos - row_sin * col_sin, row_sin * col_cos + row_cos * col_sin


def phase_kernel(core, kept, taken, row_trig, col_trig, down, up, rim, total):
    first_core = core[0] == 0
    held = kept.shape[1]
    totals = [None, None]
    for slab in range(2 * held):
        local = slab % held
        pick = lambda part: (
            jnp.where(first_core, kept[part, local], taken[part, local])
            if slab < held
            else jnp.where(first_core, taken[part, local], kept[part, local])
        )
        re, im = pick(0), pick(1)
        cosine, sine = turned(row_trig, col_trig, slab)
        a, b, c, d = re * cosine, im * sine, re * sine, im * cosine
        sums = (a - b, c + d)
        rises = (a + b, d - c)
        for part in range(2):
            down[part, slab] = sums[part]
            totals[part] = sums[part] if slab == 0 else totals[part] + sums[part]
            if slab < 2 * held - EPS_MOST:
                up[part, slab] = rises[part]
            else:
                rim[part, slab - 2 * held + EPS_MOST] = rises[part]
    for part in range(2):
        for block in range(8):
            for lane in range(2):
                tile = totals[part][8 * block : 8 * block + 8, 128 * lane : 128 * lane + 128]
                total[(8 * part + block) // 2, 2 * (block % 2) + lane] = tile


def group_kernel(parts, out, total):
    state = parts[parts.shape[0] - 1]
    out[parts.shape[0] - 1] = jnp.zeros(parts.shape[1:], f32)
    for place in range(parts.shape[0] - 2, -1, -1):
        out[place] = state
        state = state + parts[place]
    total[...] = state


def deep_kernel(sums, *refs):
    deeper, out = refs[:-1], refs[-1]
    extra = deeper[0][...]
    for other in deeper[1:]:
        extra = extra + other[...]
    for place in range(sums.shape[0]):
        out[place] = sums[place] + extra


def late_kernel(carry, down, up, rim, eps_r, eps_c, out):
    near_row = eps_r[...] == 1
    for part in range(2):
        for slab in range(SLABS):
            out[slab, 2 + part] = rim[part, slab] if slab < EPS_MOST else up[part, slab - EPS_MOST]
        for block in range(8):
            rows = slice(8 * block, 8 * block + 8)
            for lane in range(2):
                cols = slice(128 * lane, 128 * lane + 128)
                near_col = eps_c[:, cols] == 1
                below = carry[(8 * part + block) // 2, 2 * (block % 2) + lane]
                for slab in range(SLABS - 1, -1, -1):
                    here = below + down[part, slab, rows, cols]
                    out[slab, part, rows, cols] = jnp.where(near_row[rows], here, below)
                    out[slab, 4 + part, rows, cols] = jnp.where(near_col, here, below)
                    below = here
    for idle in range(SLABS, out.shape[0]):
        out[idle] = jnp.zeros(out.shape[1:], f32)


def split(value):
    high = value.astype(jnp.bfloat16)
    return high, (value - high.astype(f32)).astype(jnp.bfloat16)


def real_dot(first, second):
    dot = lambda a, b: jnp.dot(a, b, preferred_element_type=f32)
    return dot(first[0], second[0]) + (dot(first[0], second[1]) + dot(first[1], second[0]))


def complex_dot(first, second):
    p = real_dot(first[0], second[0])
    q = real_dot(first[1], second[1])
    r = real_dot(first[2], second[2])
    return p - q, r - p - q


def triple(re, im):
    return split(re), split(im), split(re + im)


def right_kernel(core, whole, far_right, part):
    half = part.shape[-1]
    step = half // 2

    def rows_of(array, line, parity):
        return [whole[:, array + part, :, line, parity].reshape(step, half) for part in range(2)]

    own = [jnp.concatenate(pair, axis=0) for pair in zip(rows_of(4, 0, core[0]), rows_of(4, 1, core[0]))]
    own = triple(*own)
    for line in range(2):
        both = triple(*rows_of(4, line, 1 - core[0]))
        for kind in range(3):
            for level in range(2):
                far_right[kind, level, line * step : line * step + step] = both[kind][level]
    for block, parity in enumerate((core[0], 1 - core[0])):
        for line in range(2):
            rows = slice(block * half + line * step, block * half + line * step + step)
            product = complex_dot(triple(*rows_of(2, line, parity)), own)
            for level in range(2):
                part[level, rows] = product[level]


def first_kernel(core, far, far_right, part, out):
    half = out.shape[-1]
    second = [(far_right[kind, 0], far_right[kind, 1]) for kind in range(3)]
    step = half // 2
    for block, parity in enumerate((core[0], 1 - core[0])):
        for line in range(2):
            rows = slice(block * half + line * step, block * half + line * step + step)
            rises = [far[:, level, :, line, parity].reshape(step, half) for level in range(2)]
            product = complex_dot(triple(*rises), second)
            both = triple(*(product[level] + part[level, rows] for level in range(2)))
            for kind in range(3):
                for level in range(2):
                    out[kind, level, rows] = both[kind][level]


def second_kernel(own, far, middle, out):
    quarter = out.shape[-1]
    half = 2 * quarter
    chips, rows = own.shape[0], own.shape[2]
    second = [(middle[kind, 0], middle[kind, 1]) for kind in range(3)]
    step = 2
    for start in range(0, chips, step):
        pieces = slice(start, start + step)
        left = [jnp.concatenate([ref[pieces, part].reshape(step * rows, half) for ref in (own, far)], axis=1) for part in range(2)]
        result = complex_dot(triple(*left), second)
        for part in range(2):
            value = result[part].reshape(step, rows, half)
            for line in range(2):
                out[line, pieces, part] = value[:, :, line * quarter : line * quarter + quarter]


def turn_kernel(scale, chips, parts, out):
    total = None
    for place in range(parts.shape[0]):
        if place % chips < SLABS:
            total = parts[place] if total is None else total + parts[place]
    turned = (jnp.concatenate([total[0], total[1]], axis=0) * scale).T
    out[...] = turned.reshape(out.shape)


def last_kernel(parts, out):
    total = parts[0]
    for place in range(1, parts.shape[0]):
        total = total + parts[place]
    turned = total.T
    rows = out.shape[1]
    out[0] = turned[:rows]
    out[1] = turned[rows:]


def body(data, wavenumbers, eps_rows, eps_cols):
    slab_count, row_count, width = data.shape[1:]
    deep = lax.axis_size("depth")
    chips = lax.axis_size("row")
    pairs = deep // 2
    half = width // 2
    place = lax.axis_index("depth")
    core = place % 2
    pair = place // 2
    total_depth = slab_count * deep
    me = core.reshape(1).astype(jnp.int32)

    planes = pairs // 2
    spot = jnp.arange(width)
    parity = jnp.where(spot < half, core, 1 - core)
    line, plane = spot % half // (half // 2), spot % (half // 2) // CHUNK
    column = ((plane * 2 + line) * 2 + parity) * CHUNK + spot % CHUNK
    chosen = (jnp.arange(width)[:, None] == column[None, :]).astype(f32)
    sorted_data = jnp.dot(data.reshape(-1, width), chosen, precision=lax.Precision.HIGHEST)
    kept = sorted_data[:, :half].reshape(2, slab_count, row_count, half)
    given = sorted_data[:, half:].reshape(2, slab_count, row_count, half)
    swap = [(i, i ^ 1) for i in range(deep)]
    taken = lax.ppermute(given, "depth", swap)

    row_waves = lax.dynamic_slice_in_dim(wavenumbers, lax.axis_index("row") * row_count, row_count)
    mine = lambda v: jnp.sum(chosen[:, :half] * v[:, None], axis=0)
    col_waves = mine(wavenumbers)
    near_cols = mine(eps_cols.astype(f32)).astype(jnp.int32).reshape(1, half)
    levels = (pair * SLABS + jnp.arange(8)).astype(f32) + 0.5
    row_phase = row_waves[:, None] * levels[None, :]
    col_phase = levels[:, None] * col_waves[None, :]
    row_trig = jnp.concatenate([jnp.cos(row_phase), jnp.sin(row_phase)], axis=1)
    col_trig = jnp.concatenate([jnp.cos(col_phase), jnp.sin(col_phase)], axis=0)
    down, up, rim, total = call(
        phase_kernel,
        [
            (2, SLABS, row_count, half),
            (2, SLABS - EPS_MOST, row_count, half),
            (2, EPS_MOST, row_count, half),
            (NEAR, 32 // NEAR, 8, 128),
        ],
        me, kept, taken, row_trig, col_trig,
        smem=(0,),
        room=10,
    )

    near = [[2 * (g * NEAR + i) + c for i in range(NEAR)] for g in range(pairs // NEAR) for c in range(2)]
    spread = lambda v, groups: lax.all_to_all(v, "depth", 0, 0, axis_index_groups=groups, tiled=True)
    seen = spread(total, near)
    sums, group = call(group_kernel, [seen.shape, seen.shape[1:]], seen)
    onward = lambda v, by: lax.ppermute(v, "depth", [(i, i - by) for i in range(by, deep)])
    deeper = [onward(group, 2 * NEAR * by) for by in (3, 1, 2)]
    rim = lax.ppermute(rim, "depth", [(i, i + 2) for i in range(deep - 2)])
    rim, *deeper = lax.optimization_barrier((rim, *deeper))
    carry = spread(call(deep_kernel, sums.shape, sums, *deeper), near)

    late = call(
        late_kernel,
        (chips, 6, row_count, half),
        carry, down, up, rim, eps_rows.reshape(row_count, 1), near_cols,
    )
    whole = lax.all_to_all(late, "row", 0, 0, tiled=True)
    up_far = lax.ppermute(whole[:, 2:4], "depth", swap)
    left_far = lax.ppermute(whole[:, :2], "depth", swap)
    shape = lambda v: v.reshape(chips, v.shape[1], row_count // 32, 2, 2, CHUNK, half)
    parts = lambda n: jax.ShapeDtypeStruct((3, 2, n, half), jnp.bfloat16)
    far_right, part = call(
        right_kernel,
        [parts(half), (2, width, half)],
        me, shape(whole),
        smem=(0,),
        flops=9 * width * width * half,
        room=12,
    )
    middle = call(
        first_kernel,
        parts(width),
        me, shape(up_far), far_right, part,
        smem=(0,),
        flops=9 * width * width * half,
        room=12,
    )
    partial = call(
        second_kernel,
        (2, chips, 2, row_count, half // 2),
        whole, left_far, middle,
        flops=18 * width * width * half,
        room=12,
    )
    in_plane = [
        [(4 * z + 2 * line + c) * chips + chip for line in range(2) for chip in range(chips)] for z in range(planes) for c in range(2)
    ]
    partial = partial.reshape(2 * chips, 2, row_count, half // 2)
    gathered = lax.all_to_all(partial, ("depth", "row"), 0, 0, axis_index_groups=in_plane, tiled=True)
    turned = call(
        lambda parts, out: turn_kernel(4.0 / total_depth, chips, parts, out),
        (planes, CHUNK, 2 * row_count),
        gathered,
    )
    ends = spread(turned, [[4 * z + k for z in range(planes)] for k in range(4)])
    return call(last_kernel, (2, row_count, CHUNK), ends)


def solution(mesh):
    in_specs = (P(None, "depth", "row", None), P(), P("row"), P())
    out_specs = P(None, "row", "depth")
    return jax.shard_map(body, mesh=mesh, in_specs=in_specs, out_specs=out_specs, check_vma=False)
```

```python
import jax
import jax.numpy as jnp
from jax import lax
from jax.experimental import pallas as pl
from jax.experimental.pallas import tpu as pltpu
from jax.sharding import PartitionSpec as P

EPS_MOST = 2
CHUNK = 8
SLABS = 6
NEAR = 8
VMEM = pl.BlockSpec(memory_space=pltpu.VMEM)
SMEM = pl.BlockSpec(memory_space=pltpu.SMEM)
HBM = pl.BlockSpec(memory_space=pltpu.HBM)
MIB = 1024 * 1024
f32 = jnp.float32


def call(kernel, out_shape, *args, scratch=(), smem=(), hbm=(), flops=0, room=6):
    single = not isinstance(out_shape, list)
    shapes = [out_shape] if single else out_shape
    shapes = [s if hasattr(s, "dtype") else jax.ShapeDtypeStruct(s, f32) for s in shapes]
    moved = sum(a.size * 4 for a in args) + sum(4 * s.size for s in shapes)
    return pl.pallas_call(
        kernel,
        out_shape=shapes[0] if single else shapes,
        in_specs=[SMEM if i in smem else HBM if i in hbm else VMEM for i in range(len(args))],
        out_specs=VMEM if single else [VMEM] * len(shapes),
        scratch_shapes=list(scratch),
        compiler_params=pltpu.CompilerParams(vmem_limit_bytes=room * MIB),
        cost_estimate=pl.CostEstimate(flops=flops, bytes_accessed=moved, transcendentals=0),
    )(*args)


def turned(row_trig, col_trig, level):
    row_cos, row_sin = row_trig[:, level : level + 1], row_trig[:, 8 + level : 9 + level]
    col_cos, col_sin = col_trig[level : level + 1, :], col_trig[8 + level : 9 + level, :]
    return row_cos * col_cos - row_sin * col_sin, row_sin * col_cos + row_cos * col_sin


def phase_kernel(core, kept, taken, row_trig, col_trig, _row, _col, down, up, rim, total):
    first_core = core[0] == 0
    held = kept.shape[1]
    totals = [None, None]
    for slab in range(2 * held):
        local = slab % held
        pick = lambda part: (
            jnp.where(first_core, kept[part, local], taken[part, local])
            if slab < held
            else jnp.where(first_core, taken[part, local], kept[part, local])
        )
        re, im = pick(0), pick(1)
        cosine, sine = turned(row_trig, col_trig, slab)
        a, b, c, d = re * cosine, im * sine, re * sine, im * cosine
        sums = (a - b, c + d)
        rises = (a + b, d - c)
        for part in range(2):
            down[part, slab] = sums[part]
            totals[part] = sums[part] if slab == 0 else totals[part] + sums[part]
            if slab < 2 * held - EPS_MOST:
                up[part, slab] = rises[part]
            else:
                rim[part, slab - 2 * held + EPS_MOST] = rises[part]
    for part in range(2):
        for block in range(8):
            for lane in range(2):
                tile = totals[part][8 * block : 8 * block + 8, 128 * lane : 128 * lane + 128]
                total[(8 * part + block) // 2, 2 * (block % 2) + lane] = tile


def group_kernel(parts, out, total):
    state = parts[parts.shape[0] - 1]
    out[parts.shape[0] - 1] = jnp.zeros(parts.shape[1:], f32)
    for place in range(parts.shape[0] - 2, -1, -1):
        out[place] = state
        state = state + parts[place]
    total[...] = state


def deep_kernel(sums, *refs):
    deeper, out = refs[:-1], refs[-1]
    extra = deeper[0][...]
    for other in deeper[1:]:
        extra = extra + other[...]
    for place in range(sums.shape[0]):
        out[place] = sums[place] + extra


def late_kernel(carry, down, up, rim, eps_r, eps_c, out):
    near_row = eps_r[...] == 1
    for part in range(2):
        for slab in range(SLABS):
            out[slab, 2 + part] = rim[part, slab] if slab < EPS_MOST else up[part, slab - EPS_MOST]
        for block in range(8):
            rows = slice(8 * block, 8 * block + 8)
            for lane in range(2):
                cols = slice(128 * lane, 128 * lane + 128)
                near_col = eps_c[:, cols] == 1.0
                below = carry[(8 * part + block) // 2, 2 * (block % 2) + lane]
                for slab in range(SLABS - 1, -1, -1):
                    here = below + down[part, slab, rows, cols]
                    out[slab, part, rows, cols] = jnp.where(near_row[rows], here, below)
                    out[slab, 4 + part, rows, cols] = jnp.where(near_col, here, below)
                    below = here
    for idle in range(SLABS, out.shape[0]):
        out[idle] = jnp.zeros(out.shape[1:], f32)


def split(value):
    high = value.astype(jnp.bfloat16)
    return high, (value - high.astype(f32)).astype(jnp.bfloat16)


def real_dot(first, second):
    dot = lambda a, b: jnp.dot(a, b, preferred_element_type=f32)
    return dot(first[0], second[0]) + (dot(first[0], second[1]) + dot(first[1], second[0]))


def complex_dot(first, second):
    p = real_dot(first[0], second[0])
    q = real_dot(first[1], second[1])
    r = real_dot(first[2], second[2])
    return p - q, r - p - q


def triple(re, im):
    return split(re), split(im), split(re + im)


def right_kernel(core, whole, far_right, part):
    half = part.shape[-1]
    step = half // 2

    def rows_of(array, line, parity):
        return [whole[:, array + part, :, line, parity].reshape(step, half) for part in range(2)]

    own = [jnp.concatenate(pair, axis=0) for pair in zip(rows_of(4, 0, core[0]), rows_of(4, 1, core[0]))]
    own = triple(*own)
    for line in range(2):
        both = triple(*rows_of(4, line, 1 - core[0]))
        for kind in range(3):
            for level in range(2):
                far_right[kind, level, line * step : line * step + step] = both[kind][level]
    for block, parity in enumerate((core[0], 1 - core[0])):
        for line in range(2):
            rows = slice(block * half + line * step, block * half + line * step + step)
            product = complex_dot(triple(*rows_of(2, line, parity)), own)
            for level in range(2):
                part[level, rows] = product[level]


def first_kernel(core, far, far_right, part, out):
    half = out.shape[-1]
    second = [(far_right[kind, 0], far_right[kind, 1]) for kind in range(3)]
    step = half // 2
    for block, parity in enumerate((core[0], 1 - core[0])):
        for line in range(2):
            rows = slice(block * half + line * step, block * half + line * step + step)
            rises = [far[:, level, :, line, parity].reshape(step, half) for level in range(2)]
            product = complex_dot(triple(*rises), second)
            both = triple(*(product[level] + part[level, rows] for level in range(2)))
            for kind in range(3):
                for level in range(2):
                    out[kind, level, rows] = both[kind][level]


def second_kernel(own, far, middle, out):
    quarter = out.shape[-1]
    half = 2 * quarter
    chips, rows = own.shape[0], own.shape[2]
    second = [(middle[kind, 0], middle[kind, 1]) for kind in range(3)]
    step = 2
    for start in range(0, chips, step):
        pieces = slice(start, start + step)
        left = [jnp.concatenate([ref[pieces, part].reshape(step * rows, half) for ref in (own, far)], axis=1) for part in range(2)]
        result = complex_dot(triple(*left), second)
        for part in range(2):
            value = result[part].reshape(step, rows, half)
            for line in range(2):
                out[line, pieces, part] = value[:, :, line * quarter : line * quarter + quarter]


def turn_kernel(scale, chips, parts, out):
    total = None
    for place in range(parts.shape[0]):
        if place % chips < SLABS:
            total = parts[place] if total is None else total + parts[place]
    turned = (jnp.concatenate([total[0], total[1]], axis=0) * scale).T
    out[...] = turned.reshape(out.shape)


def last_kernel(parts, out):
    total = parts[0]
    for place in range(1, parts.shape[0]):
        total = total + parts[place]
    rows = out.shape[2]
    out[0] = total[:, :rows]
    out[1] = total[:, rows:]


def body(data, wavenumbers, eps_rows, eps_cols):
    slab_count, row_count, width = data.shape[1:]
    deep = lax.axis_size("depth")
    chips = lax.axis_size("row")
    pairs = deep // 2
    half = width // 2
    place = lax.axis_index("depth")
    core = place % 2
    pair = place // 2
    total_depth = slab_count * deep
    me = core.reshape(1).astype(jnp.int32)

    planes = pairs // 2
    spot = jnp.arange(width)
    parity = jnp.where(spot < half, core, 1 - core)
    line, plane = spot % half // (half // 2), spot % (half // 2) // CHUNK
    column = ((plane * 2 + line) * 2 + parity) * CHUNK + spot % CHUNK
    chosen = (jnp.arange(width)[:, None] == column[None, :]).astype(f32)
    sorted_data = jnp.dot(data.reshape(-1, width), chosen, precision=lax.Precision.HIGH)
    kept = sorted_data[:, :half].reshape(2, slab_count, row_count, half)
    given = sorted_data[:, half:].reshape(2, slab_count, row_count, half)
    swap = [(i, i ^ 1) for i in range(deep)]
    taken = lax.ppermute(given, "depth", swap)

    row_waves = lax.dynamic_slice_in_dim(wavenumbers, lax.axis_index("row") * row_count, row_count)
    mine = lambda v: jnp.sum(chosen[:, :half] * v[:, None], axis=0)
    col_waves = mine(wavenumbers)
    near_cols = mine(eps_cols.astype(f32)).reshape(1, half)
    levels = (pair * SLABS + jnp.arange(8)).astype(f32) + 0.5
    row_phase = row_waves[:, None] * levels[None, :]
    col_phase = levels[:, None] * col_waves[None, :]
    row_trig = jnp.concatenate([jnp.cos(row_phase), jnp.sin(row_phase)], axis=1)
    col_trig = jnp.concatenate([jnp.cos(col_phase), jnp.sin(col_phase)], axis=0)
    row_marks = eps_rows.reshape(row_count, 1)
    down, up, rim, total = call(
        phase_kernel,
        [
            (2, SLABS, row_count, half),
            (2, SLABS - EPS_MOST, row_count, half),
            (2, EPS_MOST, row_count, half),
            (NEAR, 32 // NEAR, 8, 128),
        ],
        me, kept, taken, row_trig, col_trig, row_marks, near_cols,
        smem=(0,),
        room=10,
    )

    near = [[2 * (g * NEAR + i) + c for i in range(NEAR)] for g in range(pairs // NEAR) for c in range(2)]
    spread = lambda v, groups: lax.all_to_all(v, "depth", 0, 0, axis_index_groups=groups, tiled=True)
    seen = spread(total, near)
    sums, group = call(group_kernel, [seen.shape, seen.shape[1:]], seen)
    onward = lambda v, by: lax.ppermute(v, "depth", [(i, i - by) for i in range(by, deep)])
    deeper = [onward(group, 2 * NEAR * by) for by in (3, 1, 2)]
    rim = lax.ppermute(rim, "depth", [(i, i + 2) for i in range(deep - 2)])
    rim, *deeper = lax.optimization_barrier((rim, *deeper))
    carry = spread(call(deep_kernel, sums.shape, sums, *deeper), near)

    late = call(
        late_kernel,
        (chips, 6, row_count, half),
        carry, down, up, rim, row_marks, near_cols,
    )
    whole = lax.all_to_all(late, "row", 0, 0, tiled=True)
    up_far = lax.ppermute(whole[:, 2:4], "depth", swap)
    left_far = lax.ppermute(whole[:, :2], "depth", swap)
    shape = lambda v: v.reshape(chips, v.shape[1], row_count // 32, 2, 2, CHUNK, half)
    parts = lambda n: jax.ShapeDtypeStruct((3, 2, n, half), jnp.bfloat16)
    far_right, part = call(
        right_kernel,
        [parts(half), (2, width, half)],
        me, shape(whole),
        smem=(0,),
        flops=9 * width * width * half,
        room=12,
    )
    middle = call(
        first_kernel,
        parts(width),
        me, shape(up_far), far_right, part,
        smem=(0,),
        flops=9 * width * width * half,
        room=12,
    )
    partial = call(
        second_kernel,
        (2, chips, 2, row_count, half // 2),
        whole, left_far, middle,
        flops=18 * width * width * half,
        room=12,
    )
    in_plane = [
        [(4 * z + 2 * line + c) * chips + chip for line in range(2) for chip in range(chips)] for z in range(planes) for c in range(2)
    ]
    partial = partial.reshape(2 * chips, 2, row_count, half // 2)
    gathered = lax.all_to_all(partial, ("depth", "row"), 0, 0, axis_index_groups=in_plane, tiled=True)
    turned = call(
        lambda parts, out: turn_kernel(4.0 / total_depth, chips, parts, out),
        (planes, CHUNK, 2 * row_count),
        gathered,
    )
    ends = spread(turned, [[4 * z + k for z in range(planes)] for k in range(4)])
    return call(last_kernel, (2, CHUNK, row_count), ends).transpose(0, 2, 1)


def solution(mesh):
    in_specs = (P(None, "depth", "row", None), P(), P("row"), P())
    out_specs = P(None, "row", "depth")
    return jax.shard_map(body, mesh=mesh, in_specs=in_specs, out_specs=out_specs, check_vma=False)
```

```python
import jax
import jax.numpy as jnp
from jax import lax
from jax.experimental import pallas as pl
from jax.experimental.pallas import tpu as pltpu
from jax.sharding import PartitionSpec as P

EPS_MOST = 2
CHUNK = 8
SLABS = 6
NEAR = 8
VMEM = pl.BlockSpec(memory_space=pltpu.VMEM)
SMEM = pl.BlockSpec(memory_space=pltpu.SMEM)
HBM = pl.BlockSpec(memory_space=pltpu.HBM)
MIB = 1024 * 1024
f32 = jnp.float32


def call(kernel, out_shape, *args, scratch=(), smem=(), hbm=(), flops=0, room=6):
    single = not isinstance(out_shape, list)
    shapes = [out_shape] if single else out_shape
    shapes = [s if hasattr(s, "dtype") else jax.ShapeDtypeStruct(s, f32) for s in shapes]
    moved = sum(a.size * 4 for a in args) + sum(4 * s.size for s in shapes)
    return pl.pallas_call(
        kernel,
        out_shape=shapes[0] if single else shapes,
        in_specs=[SMEM if i in smem else HBM if i in hbm else VMEM for i in range(len(args))],
        out_specs=VMEM if single else [VMEM] * len(shapes),
        scratch_shapes=list(scratch),
        compiler_params=pltpu.CompilerParams(vmem_limit_bytes=room * MIB),
        cost_estimate=pl.CostEstimate(flops=flops, bytes_accessed=moved, transcendentals=0),
    )(*args)


def turned(row_trig, col_trig, level):
    row_cos, row_sin = row_trig[:, level : level + 1], row_trig[:, 8 + level : 9 + level]
    col_cos, col_sin = col_trig[level : level + 1, :], col_trig[8 + level : 9 + level, :]
    return row_cos * col_cos - row_sin * col_sin, row_sin * col_cos + row_cos * col_sin


def phase_kernel(core, kept, taken, row_trig, col_trig, _row, _col, down, up, rim, total):
    first_core = core[0] == 0
    held = kept.shape[1]
    totals = [None, None]
    for slab in range(2 * held):
        local = slab % held
        pick = lambda part: (
            jnp.where(first_core, kept[part, local], taken[part, local])
            if slab < held
            else jnp.where(first_core, taken[part, local], kept[part, local])
        )
        re, im = pick(0), pick(1)
        cosine, sine = turned(row_trig, col_trig, slab)
        a, b, c, d = re * cosine, im * sine, re * sine, im * cosine
        sums = (a - b, c + d)
        rises = (a + b, d - c)
        for part in range(2):
            down[part, slab] = sums[part]
            totals[part] = sums[part] if slab == 0 else totals[part] + sums[part]
            if slab < 2 * held - EPS_MOST:
                up[part, slab] = rises[part]
            else:
                rim[part, slab - 2 * held + EPS_MOST] = rises[part]
    for part in range(2):
        for block in range(8):
            for lane in range(2):
                tile = totals[part][8 * block : 8 * block + 8, 128 * lane : 128 * lane + 128]
                total[(8 * part + block) // 2, 2 * (block % 2) + lane] = tile


def group_kernel(parts, out, total):
    state = parts[parts.shape[0] - 1]
    out[parts.shape[0] - 1] = jnp.zeros(parts.shape[1:], f32)
    for place in range(parts.shape[0] - 2, -1, -1):
        out[place] = state
        state = state + parts[place]
    total[...] = state


def deep_kernel(sums, *refs):
    deeper, out = refs[:-1], refs[-1]
    extra = deeper[0][...]
    for other in deeper[1:]:
        extra = extra + other[...]
    for place in range(sums.shape[0]):
        out[place] = sums[place] + extra


def late_kernel(carry, down, up, rim, eps_r, eps_c, out):
    near_row = eps_r[...] == 1
    for part in range(2):
        for slab in range(SLABS):
            out[slab, 2 + part] = rim[part, slab] if slab < EPS_MOST else up[part, slab - EPS_MOST]
        for block in range(8):
            rows = slice(8 * block, 8 * block + 8)
            for lane in range(2):
                cols = slice(128 * lane, 128 * lane + 128)
                near_col = eps_c[:, cols] == 1.0
                below = carry[(8 * part + block) // 2, 2 * (block % 2) + lane]
                for slab in range(SLABS - 1, -1, -1):
                    here = below + down[part, slab, rows, cols]
                    out[slab, part, rows, cols] = jnp.where(near_row[rows], here, below)
                    out[slab, 4 + part, rows, cols] = jnp.where(near_col, here, below)
                    below = here
    for idle in range(SLABS, out.shape[0]):
        out[idle] = jnp.zeros(out.shape[1:], f32)


def split(value):
    high = value.astype(jnp.bfloat16)
    return high, (value - high.astype(f32)).astype(jnp.bfloat16)


def real_dot(first, second):
    dot = lambda a, b: jnp.dot(a, b, preferred_element_type=f32)
    return dot(first[0], second[0]) + (dot(first[0], second[1]) + dot(first[1], second[0]))


def complex_dot(first, second):
    p = real_dot(first[0], second[0])
    q = real_dot(first[1], second[1])
    r = real_dot(first[2], second[2])
    return p - q, r - p - q


def triple(re, im):
    return split(re), split(im), split(re + im)


def right_kernel(core, whole, far_right, part):
    half = part.shape[-1]
    step = half // 2

    def rows_of(array, line, parity):
        return [whole[:, array + part, :, line, parity].reshape(step, half) for part in range(2)]

    own = [jnp.concatenate(pair, axis=0) for pair in zip(rows_of(4, 0, core[0]), rows_of(4, 1, core[0]))]
    own = triple(*own)
    for line in range(2):
        both = triple(*rows_of(4, line, 1 - core[0]))
        for kind in range(3):
            for level in range(2):
                far_right[kind, level, line * step : line * step + step] = both[kind][level]
    for block, parity in enumerate((core[0], 1 - core[0])):
        for line in range(2):
            rows = slice(block * half + line * step, block * half + line * step + step)
            product = complex_dot(triple(*rows_of(2, line, parity)), own)
            for level in range(2):
                part[level, rows] = product[level]


def first_kernel(core, far, far_right, part, out):
    half = out.shape[-1]
    second = [(far_right[kind, 0], far_right[kind, 1]) for kind in range(3)]
    step = half // 2
    for block, parity in enumerate((core[0], 1 - core[0])):
        for line in range(2):
            rows = slice(block * half + line * step, block * half + line * step + step)
            rises = [far[:, level, :, line, parity].reshape(step, half) for level in range(2)]
            product = complex_dot(triple(*rises), second)
            both = triple(*(product[level] + part[level, rows] for level in range(2)))
            for kind in range(3):
                for level in range(2):
                    out[kind, level, rows] = both[kind][level]


def second_kernel(own, far, middle, out):
    quarter = out.shape[-1]
    half = 2 * quarter
    chips, rows = own.shape[0], own.shape[2]
    second = [(middle[kind, 0], middle[kind, 1]) for kind in range(3)]
    step = 2
    for start in range(0, chips, step):
        pieces = slice(start, start + step)
        left = [jnp.concatenate([ref[pieces, part].reshape(step * rows, half) for ref in (own, far)], axis=1) for part in range(2)]
        result = complex_dot(triple(*left), second)
        for part in range(2):
            value = result[part].reshape(step, rows, half)
            for line in range(2):
                out[line, pieces, part] = value[:, :, line * quarter : line * quarter + quarter]


def turn_kernel(scale, chips, parts, out):
    total = None
    for place in range(parts.shape[0]):
        if place % chips < SLABS:
            total = parts[place] if total is None else total + parts[place]
    turned = (jnp.concatenate([total[0], total[1]], axis=0) * scale).T
    out[...] = turned.reshape(out.shape)


def last_kernel(parts, out):
    total = parts[0]
    for place in range(1, parts.shape[0]):
        total = total + parts[place]
    rows = out.shape[2]
    out[0] = total[:, :rows]
    out[1] = total[:, rows:]


def body(data, wavenumbers, eps_rows, eps_cols):
    slab_count, row_count, width = data.shape[1:]
    deep = lax.axis_size("depth")
    chips = lax.axis_size("row")
    pairs = deep // 2
    half = width // 2
    place = lax.axis_index("depth")
    core = place % 2
    pair = place // 2
    total_depth = slab_count * deep
    me = core.reshape(1).astype(jnp.int32)

    planes = pairs // 2
    spot = jnp.arange(width)
    parity = jnp.where(spot < half, core, 1 - core)
    line, plane = spot % half // (half // 2), spot % (half // 2) // CHUNK
    column = ((plane * 2 + line) * 2 + parity) * CHUNK + spot % CHUNK
    chosen = (jnp.arange(width)[:, None] == column[None, :]).astype(f32)
    rows = data.reshape(-1, width)
    pick = lambda columns: jnp.dot(rows, columns, precision=lax.Precision.HIGH).reshape(2, slab_count, row_count, half)
    given = pick(chosen[:, half:])
    swap = [(i, i ^ 1) for i in range(deep)]
    taken = lax.ppermute(given, "depth", swap)
    kept = pick(chosen[:, :half])

    row_waves = lax.dynamic_slice_in_dim(wavenumbers, lax.axis_index("row") * row_count, row_count)
    mine = lambda v: jnp.sum(chosen[:, :half] * v[:, None], axis=0)
    col_waves = mine(wavenumbers)
    near_cols = mine(eps_cols.astype(f32)).reshape(1, half)
    levels = (pair * SLABS + jnp.arange(8)).astype(f32) + 0.5
    row_phase = row_waves[:, None] * levels[None, :]
    col_phase = levels[:, None] * col_waves[None, :]
    row_trig = jnp.concatenate([jnp.cos(row_phase), jnp.sin(row_phase)], axis=1)
    col_trig = jnp.concatenate([jnp.cos(col_phase), jnp.sin(col_phase)], axis=0)
    row_marks = eps_rows.reshape(row_count, 1)
    down, up, rim, total = call(
        phase_kernel,
        [
            (2, SLABS, row_count, half),
            (2, SLABS - EPS_MOST, row_count, half),
            (2, EPS_MOST, row_count, half),
            (NEAR, 32 // NEAR, 8, 128),
        ],
        me, kept, taken, row_trig, col_trig, row_marks, near_cols,
        smem=(0,),
        room=10,
    )

    near = [[2 * (g * NEAR + i) + c for i in range(NEAR)] for g in range(pairs // NEAR) for c in range(2)]
    spread = lambda v, groups: lax.all_to_all(v, "depth", 0, 0, axis_index_groups=groups, tiled=True)
    seen = spread(total, near)
    sums, group = call(group_kernel, [seen.shape, seen.shape[1:]], seen)
    onward = lambda v, by: lax.ppermute(v, "depth", [(i, i - by) for i in range(by, deep)])
    deeper = [onward(group, 2 * NEAR * by) for by in (3, 1, 2)]
    rim = lax.ppermute(rim, "depth", [(i, i + 2) for i in range(deep - 2)])
    rim, *deeper = lax.optimization_barrier((rim, *deeper))
    carry = spread(call(deep_kernel, sums.shape, sums, *deeper), near)

    late = call(
        late_kernel,
        (chips, 6, row_count, half),
        carry, down, up, rim, row_marks, near_cols,
    )
    whole = lax.all_to_all(late, "row", 0, 0, tiled=True)
    up_far = lax.ppermute(whole[:, 2:4], "depth", swap)
    left_far = lax.ppermute(whole[:, :2], "depth", swap)
    shape = lambda v: v.reshape(chips, v.shape[1], row_count // 32, 2, 2, CHUNK, half)
    parts = lambda n: jax.ShapeDtypeStruct((3, 2, n, half), jnp.bfloat16)
    far_right, part = call(
        right_kernel,
        [parts(half), (2, width, half)],
        me, shape(whole),
        smem=(0,),
        flops=9 * width * width * half,
        room=12,
    )
    middle = call(
        first_kernel,
        parts(width),
        me, shape(up_far), far_right, part,
        smem=(0,),
        flops=9 * width * width * half,
        room=12,
    )
    partial = call(
        second_kernel,
        (2, chips, 2, row_count, half // 2),
        whole, left_far, middle,
        flops=18 * width * width * half,
        room=12,
    )
    in_plane = [
        [(4 * z + 2 * line + c) * chips + chip for line in range(2) for chip in range(chips)] for z in range(planes) for c in range(2)
    ]
    partial = partial.reshape(2 * chips, 2, row_count, half // 2)
    gathered = lax.all_to_all(partial, ("depth", "row"), 0, 0, axis_index_groups=in_plane, tiled=True)
    turned = call(
        lambda parts, out: turn_kernel(4.0 / total_depth, chips, parts, out),
        (planes, CHUNK, 2 * row_count),
        gathered,
    )
    ends = spread(turned, [[4 * z + k for z in range(planes)] for k in range(4)])
    return call(last_kernel, (2, CHUNK, row_count), ends).transpose(0, 2, 1)


def solution(mesh):
    in_specs = (P(None, "depth", "row", None), P(), P("row"), P())
    out_specs = P(None, "row", "depth")
    return jax.shard_map(body, mesh=mesh, in_specs=in_specs, out_specs=out_specs, check_vma=False)
```

```python
import jax
import jax.numpy as jnp
from jax import lax
from jax.experimental import pallas as pl
from jax.experimental.pallas import tpu as pltpu
from jax.sharding import PartitionSpec as P

EPS_MOST = 2
CHUNK = 8
SLABS = 6
NEAR = 8
VMEM = pl.BlockSpec(memory_space=pltpu.VMEM)
SMEM = pl.BlockSpec(memory_space=pltpu.SMEM)
HBM = pl.BlockSpec(memory_space=pltpu.HBM)
MIB = 1024 * 1024
f32 = jnp.float32


def call(kernel, out_shape, *args, scratch=(), smem=(), hbm=(), flops=0, room=6):
    single = not isinstance(out_shape, list)
    shapes = [out_shape] if single else out_shape
    shapes = [s if hasattr(s, "dtype") else jax.ShapeDtypeStruct(s, f32) for s in shapes]
    moved = sum(a.size * 4 for a in args) + sum(4 * s.size for s in shapes)
    return pl.pallas_call(
        kernel,
        out_shape=shapes[0] if single else shapes,
        in_specs=[SMEM if i in smem else HBM if i in hbm else VMEM for i in range(len(args))],
        out_specs=VMEM if single else [VMEM] * len(shapes),
        scratch_shapes=list(scratch),
        compiler_params=pltpu.CompilerParams(vmem_limit_bytes=room * MIB),
        cost_estimate=pl.CostEstimate(flops=flops, bytes_accessed=moved, transcendentals=0),
    )(*args)


def turned(row_trig, col_trig, level):
    row_cos, row_sin = row_trig[:, level : level + 1], row_trig[:, 8 + level : 9 + level]
    col_cos, col_sin = col_trig[level : level + 1, :], col_trig[8 + level : 9 + level, :]
    return row_cos * col_cos - row_sin * col_sin, row_sin * col_cos + row_cos * col_sin


def rotations(core, kept, taken, row_trig, col_trig):
    held = kept.shape[1]
    for slab in range(2 * held):
        first, second = (kept, taken) if slab < held else (taken, kept)
        re, im = (jnp.where(core[0] == 0, first[part, slab % held], second[part, slab % held]) for part in range(2))
        yield (slab, re, im) + turned(row_trig, col_trig, slab)


def total_kernel(core, kept, taken, row_trig, col_trig, _row, _col, total):
    totals = [None, None]
    for slab, re, im, cosine, sine in rotations(core, kept, taken, row_trig, col_trig):
        for part, value in enumerate((re * cosine - im * sine, re * sine + im * cosine)):
            totals[part] = value if slab == 0 else totals[part] + value
    for part in range(2):
        for block in range(8):
            for lane in range(2):
                tile = totals[part][8 * block : 8 * block + 8, 128 * lane : 128 * lane + 128]
                total[(8 * part + block) // 2, 2 * (block % 2) + lane] = tile


def phase_kernel(core, kept, taken, row_trig, col_trig, down, up, rim):
    risen = up.shape[1]
    for slab, re, im, cosine, sine in rotations(core, kept, taken, row_trig, col_trig):
        a, b, c, d = re * cosine, im * sine, re * sine, im * cosine
        for part, (fall, rise) in enumerate(((a - b, a + b), (c + d, d - c))):
            down[part, slab] = fall
            if slab < risen:
                up[part, slab] = rise
            else:
                rim[part, slab - risen] = rise


def group_kernel(parts, out, total):
    state = parts[parts.shape[0] - 1]
    out[parts.shape[0] - 1] = jnp.zeros(parts.shape[1:], f32)
    for place in range(parts.shape[0] - 2, -1, -1):
        out[place] = state
        state = state + parts[place]
    total[...] = state


def deep_kernel(sums, *refs):
    deeper, out = refs[:-1], refs[-1]
    extra = deeper[0][...]
    for other in deeper[1:]:
        extra = extra + other[...]
    for place in range(sums.shape[0]):
        out[place] = sums[place] + extra


def late_kernel(carry, down, up, rim, eps_r, eps_c, out):
    near_row = eps_r[...] == 1
    for part in range(2):
        for slab in range(SLABS):
            out[slab, 2 + part] = rim[part, slab] if slab < EPS_MOST else up[part, slab - EPS_MOST]
        for block in range(8):
            rows = slice(8 * block, 8 * block + 8)
            for lane in range(2):
                cols = slice(128 * lane, 128 * lane + 128)
                near_col = eps_c[:, cols] == 1.0
                below = carry[(8 * part + block) // 2, 2 * (block % 2) + lane]
                for slab in range(SLABS - 1, -1, -1):
                    here = below + down[part, slab, rows, cols]
                    out[slab, part, rows, cols] = jnp.where(near_row[rows], here, below)
                    out[slab, 4 + part, rows, cols] = jnp.where(near_col, here, below)
                    below = here
    for idle in range(SLABS, out.shape[0]):
        out[idle] = jnp.zeros(out.shape[1:], f32)


def split(value):
    high = value.astype(jnp.bfloat16)
    return high, (value - high.astype(f32)).astype(jnp.bfloat16)


def real_dot(first, second):
    dot = lambda a, b: jnp.dot(a, b, preferred_element_type=f32)
    return dot(first[0], second[0]) + (dot(first[0], second[1]) + dot(first[1], second[0]))


def complex_dot(first, second):
    p = real_dot(first[0], second[0])
    q = real_dot(first[1], second[1])
    r = real_dot(first[2], second[2])
    return p - q, r - p - q


def triple(re, im):
    return split(re), split(im), split(re + im)


def right_kernel(core, whole, far_right, part):
    half = part.shape[-1]
    step = half // 2

    def rows_of(array, line, parity):
        return [whole[:, array + part, :, line, parity].reshape(step, half) for part in range(2)]

    own = [jnp.concatenate(pair, axis=0) for pair in zip(rows_of(4, 0, core[0]), rows_of(4, 1, core[0]))]
    own = triple(*own)
    for line in range(2):
        both = triple(*rows_of(4, line, 1 - core[0]))
        for kind in range(3):
            for level in range(2):
                far_right[kind, level, line * step : line * step + step] = both[kind][level]
    for block, parity in enumerate((core[0], 1 - core[0])):
        for line in range(2):
            rows = slice(block * half + line * step, block * half + line * step + step)
            product = complex_dot(triple(*rows_of(2, line, parity)), own)
            for level in range(2):
                part[level, rows] = product[level]


def first_kernel(core, far, far_right, part, out):
    half = out.shape[-1]
    second = [(far_right[kind, 0], far_right[kind, 1]) for kind in range(3)]
    step = half // 2
    for block, parity in enumerate((core[0], 1 - core[0])):
        for line in range(2):
            rows = slice(block * half + line * step, block * half + line * step + step)
            rises = [far[:, level, :, line, parity].reshape(step, half) for level in range(2)]
            product = complex_dot(triple(*rises), second)
            both = triple(*(product[level] + part[level, rows] for level in range(2)))
            for kind in range(3):
                for level in range(2):
                    out[kind, level, rows] = both[kind][level]


def second_kernel(own, far, middle, out):
    quarter = out.shape[-1]
    half = 2 * quarter
    chips, rows = own.shape[0], own.shape[2]
    second = [(middle[kind, 0], middle[kind, 1]) for kind in range(3)]
    step = 2
    for start in range(0, chips, step):
        pieces = slice(start, start + step)
        left = [jnp.concatenate([ref[pieces, part].reshape(step * rows, half) for ref in (own, far)], axis=1) for part in range(2)]
        result = complex_dot(triple(*left), second)
        for part in range(2):
            value = result[part].reshape(step, rows, half)
            for line in range(2):
                out[line, pieces, part] = value[:, :, line * quarter : line * quarter + quarter]


def turn_kernel(scale, chips, parts, out):
    total = None
    for place in range(parts.shape[0]):
        if place % chips < SLABS:
            total = parts[place] if total is None else total + parts[place]
    turned = (jnp.concatenate([total[0], total[1]], axis=0) * scale).T
    out[...] = turned.reshape(out.shape)


def last_kernel(parts, out):
    total = parts[0]
    for place in range(1, parts.shape[0]):
        total = total + parts[place]
    rows = out.shape[2]
    out[0] = total[:, :rows]
    out[1] = total[:, rows:]


def body(data, wavenumbers, eps_rows, eps_cols):
    slab_count, row_count, width = data.shape[1:]
    deep = lax.axis_size("depth")
    chips = lax.axis_size("row")
    pairs = deep // 2
    half = width // 2
    place = lax.axis_index("depth")
    core = place % 2
    pair = place // 2
    total_depth = slab_count * deep
    me = core.reshape(1).astype(jnp.int32)

    planes = pairs // 2
    spot = jnp.arange(width)
    parity = jnp.where(spot < half, core, 1 - core)
    line, plane = spot % half // (half // 2), spot % (half // 2) // CHUNK
    column = ((plane * 2 + line) * 2 + parity) * CHUNK + spot % CHUNK
    chosen = (jnp.arange(width)[:, None] == column[None, :]).astype(f32)
    sorted_data = jnp.dot(data.reshape(-1, width), chosen, precision=lax.Precision.HIGH)
    kept = sorted_data[:, :half].reshape(2, slab_count, row_count, half)
    given = sorted_data[:, half:].reshape(2, slab_count, row_count, half)
    swap = [(i, i ^ 1) for i in range(deep)]
    taken = lax.ppermute(given, "depth", swap)

    row_waves = lax.dynamic_slice_in_dim(wavenumbers, lax.axis_index("row") * row_count, row_count)
    mine = lambda v: jnp.sum(chosen[:, :half] * v[:, None], axis=0)
    col_waves = mine(wavenumbers)
    near_cols = mine(eps_cols.astype(f32)).reshape(1, half)
    levels = (pair * SLABS + jnp.arange(8)).astype(f32) + 0.5
    row_phase = row_waves[:, None] * levels[None, :]
    col_phase = levels[:, None] * col_waves[None, :]
    row_trig = jnp.concatenate([jnp.cos(row_phase), jnp.sin(row_phase)], axis=1)
    col_trig = jnp.concatenate([jnp.cos(col_phase), jnp.sin(col_phase)], axis=0)
    row_marks = eps_rows.reshape(row_count, 1)
    held = (me, kept, taken, row_trig, col_trig)
    total = call(total_kernel, (NEAR, 32 // NEAR, 8, 128), *held, row_marks, near_cols, smem=(0,))
    down, up, rim = call(
        phase_kernel,
        [
            (2, SLABS, row_count, half),
            (2, SLABS - EPS_MOST, row_count, half),
            (2, EPS_MOST, row_count, half),
        ],
        *held,
        smem=(0,),
        room=10,
    )

    near = [[2 * (g * NEAR + i) + c for i in range(NEAR)] for g in range(pairs // NEAR) for c in range(2)]
    spread = lambda v, groups: lax.all_to_all(v, "depth", 0, 0, axis_index_groups=groups, tiled=True)
    seen = spread(total, near)
    sums, group = call(group_kernel, [seen.shape, seen.shape[1:]], seen)
    onward = lambda v, by: lax.ppermute(v, "depth", [(i, i - by) for i in range(by, deep)])
    deeper = [onward(group, 2 * NEAR * by) for by in (3, 1, 2)]
    rim = lax.ppermute(rim, "depth", [(i, i + 2) for i in range(deep - 2)])
    rim, *deeper = lax.optimization_barrier((rim, *deeper))
    carry = spread(call(deep_kernel, sums.shape, sums, *deeper), near)

    late = call(
        late_kernel,
        (chips, 6, row_count, half),
        carry, down, up, rim, row_marks, near_cols,
    )
    whole = lax.all_to_all(late, "row", 0, 0, tiled=True)
    up_far = lax.ppermute(whole[:, 2:4], "depth", swap)
    left_far = lax.ppermute(whole[:, :2], "depth", swap)
    shape = lambda v: v.reshape(chips, v.shape[1], row_count // 32, 2, 2, CHUNK, half)
    parts = lambda n: jax.ShapeDtypeStruct((3, 2, n, half), jnp.bfloat16)
    far_right, part = call(
        right_kernel,
        [parts(half), (2, width, half)],
        me, shape(whole),
        smem=(0,),
        flops=9 * width * width * half,
        room=12,
    )
    middle = call(
        first_kernel,
        parts(width),
        me, shape(up_far), far_right, part,
        smem=(0,),
        flops=9 * width * width * half,
        room=12,
    )
    partial = call(
        second_kernel,
        (2, chips, 2, row_count, half // 2),
        whole, left_far, middle,
        flops=18 * width * width * half,
        room=12,
    )
    in_plane = [
        [(4 * z + 2 * line + c) * chips + chip for line in range(2) for chip in range(chips)] for z in range(planes) for c in range(2)
    ]
    partial = partial.reshape(2 * chips, 2, row_count, half // 2)
    gathered = lax.all_to_all(partial, ("depth", "row"), 0, 0, axis_index_groups=in_plane, tiled=True)
    turned = call(
        lambda parts, out: turn_kernel(4.0 / total_depth, chips, parts, out),
        (planes, CHUNK, 2 * row_count),
        gathered,
    )
    ends = spread(turned, [[4 * z + k for z in range(planes)] for k in range(4)])
    return call(last_kernel, (2, CHUNK, row_count), ends).transpose(0, 2, 1)


def solution(mesh):
    in_specs = (P(None, "depth", "row", None), P(), P("row"), P())
    out_specs = P(None, "row", "depth")
    return jax.shard_map(body, mesh=mesh, in_specs=in_specs, out_specs=out_specs, check_vma=False)
```

```python
import jax
import jax.numpy as jnp
from jax import lax
from jax.experimental import pallas as pl
from jax.experimental.pallas import tpu as pltpu
from jax.sharding import PartitionSpec as P

EPS_MOST = 2
CHUNK = 8
SLABS = 6
NEAR = 8
VMEM = pl.BlockSpec(memory_space=pltpu.VMEM)
SMEM = pl.BlockSpec(memory_space=pltpu.SMEM)
HBM = pl.BlockSpec(memory_space=pltpu.HBM)
MIB = 1024 * 1024
f32 = jnp.float32


def call(kernel, out_shape, *args, scratch=(), smem=(), hbm=(), flops=0, room=6):
    single = not isinstance(out_shape, list)
    shapes = [out_shape] if single else out_shape
    shapes = [s if hasattr(s, "dtype") else jax.ShapeDtypeStruct(s, f32) for s in shapes]
    moved = sum(a.size * 4 for a in args) + sum(4 * s.size for s in shapes)
    return pl.pallas_call(
        kernel,
        out_shape=shapes[0] if single else shapes,
        in_specs=[SMEM if i in smem else HBM if i in hbm else VMEM for i in range(len(args))],
        out_specs=VMEM if single else [VMEM] * len(shapes),
        scratch_shapes=list(scratch),
        compiler_params=pltpu.CompilerParams(vmem_limit_bytes=room * MIB),
        cost_estimate=pl.CostEstimate(flops=flops, bytes_accessed=moved, transcendentals=0),
    )(*args)


def turned(row_trig, col_trig, level):
    row_cos, row_sin = row_trig[:, level : level + 1], row_trig[:, 8 + level : 9 + level]
    col_cos, col_sin = col_trig[level : level + 1, :], col_trig[8 + level : 9 + level, :]
    return row_cos * col_cos - row_sin * col_sin, row_sin * col_cos + row_cos * col_sin


def rotations(core, kept, taken, row_trig, col_trig):
    held = kept.shape[1]
    for slab in range(2 * held):
        first, second = (kept, taken) if slab < held else (taken, kept)
        re, im = (jnp.where(core[0] == 0, first[part, slab % held], second[part, slab % held]) for part in range(2))
        yield (slab, re, im) + turned(row_trig, col_trig, slab)


def total_kernel(core, kept, taken, row_trig, col_trig, _row, _col, total):
    totals = [None, None]
    for slab, re, im, cosine, sine in rotations(core, kept, taken, row_trig, col_trig):
        for part, value in enumerate((re * cosine - im * sine, re * sine + im * cosine)):
            totals[part] = value if slab == 0 else totals[part] + value
    for part in range(2):
        for block in range(8):
            for lane in range(2):
                tile = totals[part][8 * block : 8 * block + 8, 128 * lane : 128 * lane + 128]
                total[(8 * part + block) // 2, 2 * (block % 2) + lane] = tile


def phase_kernel(core, kept, taken, row_trig, col_trig, down, up, rim):
    risen = up.shape[1]
    for slab, re, im, cosine, sine in rotations(core, kept, taken, row_trig, col_trig):
        a, b, c, d = re * cosine, im * sine, re * sine, im * cosine
        for part, (fall, rise) in enumerate(((a - b, a + b), (c + d, d - c))):
            down[part, slab] = fall
            if slab < risen:
                up[part, slab] = rise
            else:
                rim[part, slab - risen] = rise


def group_kernel(parts, out, total):
    state = parts[parts.shape[0] - 1]
    out[parts.shape[0] - 1] = jnp.zeros(parts.shape[1:], f32)
    for place in range(parts.shape[0] - 2, -1, -1):
        out[place] = state
        state = state + parts[place]
    total[...] = state


def deep_kernel(sums, *refs):
    deeper, out = refs[:-1], refs[-1]
    extra = deeper[0][...]
    for other in deeper[1:]:
        extra = extra + other[...]
    for place in range(sums.shape[0]):
        out[place] = sums[place] + extra


def late_kernel(carry, down, up, rim, eps_r, eps_c, out):
    near_row = eps_r[...] == 1
    for part in range(2):
        for slab in range(SLABS):
            out[slab, 2 + part] = rim[part, slab] if slab < EPS_MOST else up[part, slab - EPS_MOST]
        for block in range(8):
            rows = slice(8 * block, 8 * block + 8)
            for lane in range(2):
                cols = slice(128 * lane, 128 * lane + 128)
                near_col = eps_c[:, cols] == 1.0
                below = carry[(8 * part + block) // 2, 2 * (block % 2) + lane]
                for slab in range(SLABS - 1, -1, -1):
                    here = below + down[part, slab, rows, cols]
                    out[slab, part, rows, cols] = jnp.where(near_row[rows], here, below)
                    out[slab, 4 + part, rows, cols] = jnp.where(near_col, here, below)
                    below = here
    for idle in range(SLABS, out.shape[0]):
        out[idle] = jnp.zeros(out.shape[1:], f32)


def split(value):
    high = value.astype(jnp.bfloat16)
    return high, (value - high.astype(f32)).astype(jnp.bfloat16)


def real_dot(first, second):
    dot = lambda a, b: jnp.dot(a, b, preferred_element_type=f32)
    return dot(first[0], second[0]) + (dot(first[0], second[1]) + dot(first[1], second[0]))


def complex_dot(first, second):
    p = real_dot(first[0], second[0])
    q = real_dot(first[1], second[1])
    r = real_dot(first[2], second[2])
    return p - q, r - p - q


def triple(re, im):
    return split(re), split(im), split(re + im)


def right_kernel(core, whole, far_right, part):
    half = part.shape[-1]
    step = half // 2

    def rows_of(array, line, parity):
        return [whole[:, array + part, :, line, parity].reshape(step, half) for part in range(2)]

    own = [jnp.concatenate(pair, axis=0) for pair in zip(rows_of(4, 0, core[0]), rows_of(4, 1, core[0]))]
    own = triple(*own)
    for line in range(2):
        both = triple(*rows_of(4, line, 1 - core[0]))
        for kind in range(3):
            for level in range(2):
                far_right[kind, level, line * step : line * step + step] = both[kind][level]
    for block, parity in enumerate((core[0], 1 - core[0])):
        for line in range(2):
            rows = slice(block * half + line * step, block * half + line * step + step)
            product = complex_dot(triple(*rows_of(2, line, parity)), own)
            for level in range(2):
                part[level, rows] = product[level]


def first_kernel(core, far, far_right, part, out):
    half = out.shape[-1]
    second = [(far_right[kind, 0], far_right[kind, 1]) for kind in range(3)]
    step = half // 2
    for block, parity in enumerate((core[0], 1 - core[0])):
        for line in range(2):
            rows = slice(block * half + line * step, block * half + line * step + step)
            rises = [far[:, 2 + level, :, line, parity].reshape(step, half) for level in range(2)]
            product = complex_dot(triple(*rises), second)
            both = triple(*(product[level] + part[level, rows] for level in range(2)))
            for kind in range(3):
                for level in range(2):
                    out[kind, level, rows] = both[kind][level]


def second_kernel(own, far, middle, out):
    quarter = out.shape[-1]
    half = 2 * quarter
    chips, rows = own.shape[0], own.shape[2]
    second = [(middle[kind, 0], middle[kind, 1]) for kind in range(3)]
    step = 2
    for start in range(0, chips, step):
        pieces = slice(start, start + step)
        left = [jnp.concatenate([ref[pieces, part].reshape(step * rows, half) for ref in (own, far)], axis=1) for part in range(2)]
        result = complex_dot(triple(*left), second)
        for part in range(2):
            value = result[part].reshape(step, rows, half)
            for line in range(2):
                out[line, pieces, part] = value[:, :, line * quarter : line * quarter + quarter]


def turn_kernel(scale, chips, parts, out):
    total = None
    for place in range(parts.shape[0]):
        if place % chips < SLABS:
            total = parts[place] if total is None else total + parts[place]
    turned = (jnp.concatenate([total[0], total[1]], axis=0) * scale).T
    out[...] = turned.reshape(out.shape)


def last_kernel(parts, out):
    total = parts[0]
    for place in range(1, parts.shape[0]):
        total = total + parts[place]
    rows = out.shape[2]
    out[0] = total[:, :rows]
    out[1] = total[:, rows:]


def body(data, wavenumbers, eps_rows, eps_cols):
    slab_count, row_count, width = data.shape[1:]
    deep = lax.axis_size("depth")
    chips = lax.axis_size("row")
    pairs = deep // 2
    half = width // 2
    place = lax.axis_index("depth")
    core = place % 2
    pair = place // 2
    total_depth = slab_count * deep
    me = core.reshape(1).astype(jnp.int32)

    planes = pairs // 2
    spot = jnp.arange(width)
    parity = jnp.where(spot < half, core, 1 - core)
    line, plane = spot % half // (half // 2), spot % (half // 2) // CHUNK
    column = ((plane * 2 + line) * 2 + parity) * CHUNK + spot % CHUNK
    chosen = (jnp.arange(width)[:, None] == column[None, :]).astype(f32)
    sorted_data = jnp.dot(data.reshape(-1, width), chosen, precision=lax.Precision.HIGH)
    kept = sorted_data[:, :half].reshape(2, slab_count, row_count, half)
    given = sorted_data[:, half:].reshape(2, slab_count, row_count, half)
    swap = [(i, i ^ 1) for i in range(deep)]
    taken = lax.ppermute(given, "depth", swap)

    row_waves = lax.dynamic_slice_in_dim(wavenumbers, lax.axis_index("row") * row_count, row_count)
    mine = lambda v: jnp.sum(chosen[:, :half] * v[:, None], axis=0)
    col_waves = mine(wavenumbers)
    near_cols = mine(eps_cols.astype(f32)).reshape(1, half)
    levels = (pair * SLABS + jnp.arange(8)).astype(f32) + 0.5
    row_phase = row_waves[:, None] * levels[None, :]
    col_phase = levels[:, None] * col_waves[None, :]
    row_trig = jnp.concatenate([jnp.cos(row_phase), jnp.sin(row_phase)], axis=1)
    col_trig = jnp.concatenate([jnp.cos(col_phase), jnp.sin(col_phase)], axis=0)
    row_marks = eps_rows.reshape(row_count, 1)
    held = (me, kept, taken, row_trig, col_trig)
    total = call(total_kernel, (NEAR, 32 // NEAR, 8, 128), *held, row_marks, near_cols, smem=(0,))
    down, up, rim = call(
        phase_kernel,
        [
            (2, SLABS, row_count, half),
            (2, SLABS - EPS_MOST, row_count, half),
            (2, EPS_MOST, row_count, half),
        ],
        *held,
        smem=(0,),
        room=10,
    )

    near = [[2 * (g * NEAR + i) + c for i in range(NEAR)] for g in range(pairs // NEAR) for c in range(2)]
    spread = lambda v, groups: lax.all_to_all(v, "depth", 0, 0, axis_index_groups=groups, tiled=True)
    seen = spread(total, near)
    sums, group = call(group_kernel, [seen.shape, seen.shape[1:]], seen)
    onward = lambda v, by: lax.ppermute(v, "depth", [(i, i - by) for i in range(by, deep)])
    deeper = [onward(group, 2 * NEAR * by) for by in (3, 1, 2)]
    rim = lax.ppermute(rim, "depth", [(i, i + 2) for i in range(deep - 2)])
    rim, *deeper = lax.optimization_barrier((rim, *deeper))
    carry = spread(call(deep_kernel, sums.shape, sums, *deeper), near)

    late = call(
        late_kernel,
        (chips, 6, row_count, half),
        carry, down, up, rim, row_marks, near_cols,
    )
    whole = lax.all_to_all(late, "row", 0, 0, tiled=True)
    other = lax.ppermute(whole[:, :4], "depth", swap)
    shape = lambda v: v.reshape(chips, v.shape[1], row_count // 32, 2, 2, CHUNK, half)
    parts = lambda n: jax.ShapeDtypeStruct((3, 2, n, half), jnp.bfloat16)
    far_right, part = call(
        right_kernel,
        [parts(half), (2, width, half)],
        me, shape(whole),
        smem=(0,),
        flops=9 * width * width * half,
        room=12,
    )
    middle = call(
        first_kernel,
        parts(width),
        me, shape(other), far_right, part,
        smem=(0,),
        flops=9 * width * width * half,
        room=12,
    )
    partial = call(
        second_kernel,
        (2, chips, 2, row_count, half // 2),
        whole, other, middle,
        flops=18 * width * width * half,
        room=12,
    )
    in_plane = [
        [(4 * z + 2 * line + c) * chips + chip for line in range(2) for chip in range(chips)] for z in range(planes) for c in range(2)
    ]
    partial = partial.reshape(2 * chips, 2, row_count, half // 2)
    gathered = lax.all_to_all(partial, ("depth", "row"), 0, 0, axis_index_groups=in_plane, tiled=True)
    turned = call(
        lambda parts, out: turn_kernel(4.0 / total_depth, chips, parts, out),
        (planes, CHUNK, 2 * row_count),
        gathered,
    )
    ends = spread(turned, [[4 * z + k for z in range(planes)] for k in range(4)])
    return call(last_kernel, (2, CHUNK, row_count), ends).transpose(0, 2, 1)


def solution(mesh):
    in_specs = (P(None, "depth", "row", None), P(), P("row"), P())
    out_specs = P(None, "row", "depth")
    return jax.shard_map(body, mesh=mesh, in_specs=in_specs, out_specs=out_specs, check_vma=False)
```
